512 devices in a mesh: member: 8 (over y), sx: 8 (over z_hi, core), sy: 8 (over z_lo, x).
Axes of the slice: x: 4, y: 8, z: 8 (z_hi: 4, z_lo: 2; z = z_hi * 2 + z_lo), core: 2. Of those that a mesh axis runs over, the one named last changes fastest.
Arguments:
- states: bfloat16 [8, 256, 128, 512], P('member', 'sx', 'sy'), may hold values from -6 to 6
- noises: float32 [8, 32], P('member'), may hold values from -4 to 4
- codes: int32 [256, 128, 6], P('sx', 'sy'), may hold values from 0 to 8
- target: bfloat16 [256, 128, 128], P('sx', 'sy'), may hold values from -6 to 6
- w_self: bfloat16 [2, 512, 512], replicated, may hold values from -0.25 to 0.25
- w_nbr: bfloat16 [2, 512, 512], replicated, may hold values from -0.25 to 0.25
- w_out: bfloat16 [2, 512, 512], replicated, may hold values from -0.25 to 0.25
- w_scale: float32 [2, 32, 512], replicated, may hold values from -0.5 to 0.5
- w_shift: float32 [2, 32, 512], replicated, may hold values from -0.5 to 0.5
- w_dec: bfloat16 [512, 128], replicated, may hold values from -0.25 to 0.25
Outputs:
- preds: bfloat16 [8, 256, 128, 128], P('member', 'sx', 'sy')
- ranked_probability_score: float32 [256, 128, 128], P('sx', 'sy')
The draws below stay inside these ranges and needn't reach their ends.
All inputs are finite; a program needn't handle non-finite values.
Results may differ from the reference program's by a relative error of at most 0.009.
Values may be sent and summed in bfloat16 or wider, within the bound.
No kernel may reach another device: no remote copies, remote signals or barrier semaphores. Data moves between devices by JAX's collectives and lax.ppermute only.
A program may use at most 64 MiB of HBM per device.

```python
import jax
import jax.numpy as jnp
from jax import lax

D = 512
NOISE = 32
VARS = 128
DEGREE = 6
DEPTH_COUNT = 2
MEMBERS = 8
NX = 256
NY = 128


def with_ends(result, stream_key, least, top_value):
    longest = result.shape.index(max(result.shape))
    spots = []
    for shift in (0, 1):
        where = [jax.random.randint(jax.random.fold_in(stream_key, axis), (), 0, length) for axis, length in enumerate(result.shape)]
        where[longest] = (where[longest] + shift) % result.shape[longest]
        spots.append(tuple(where))
    return result.at[spots[0]].set(least).at[spots[1]].set(top_value)


def block_scale(rng, dims, shards, low, top_value):
    def one(dim, blocks):
        steps = jax.random.uniform(jax.random.fold_in(jax.random.fold_in(rng, 6), dim), (blocks,), jnp.float32, low / len(shards), top_value / len(shards))
        return jnp.repeat(jnp.exp(steps), dims[dim] // blocks).reshape((-1,) + (1,) * (len(dims) - dim - 1))

    factor_of = one(*shards[0])
    for cut in shards[1:]:
        factor_of = factor_of * one(*cut)
    return factor_of


def gaussian(stream_key, shape, scale, bound, cuts=(), held_as=jnp.bfloat16):
    array = jax.random.normal(stream_key, shape, jnp.float32) * scale
    if len(cuts) > 0:
        array = block_scale(stream_key, shape, cuts, -0.22, 0.18) * array
    return jnp.clip(array, min=-bound, max=bound).astype(held_as)


def setup_inputs(seed: int = 0) -> dict:
    streams_of = jax.random.split(jax.random.key(seed), 11)
    states = gaussian(streams_of[0], (MEMBERS, NX, NY, D), 1.0, 6.0, ((0, 8), (1, 8), (2, 8)))
    noises = gaussian(streams_of[1], (MEMBERS, NOISE), 1.0, 4.0, ((0, 8),), jnp.float32)
    codes = with_ends(jax.random.randint(streams_of[2], (NX, NY, DEGREE), 0, 9), jax.random.fold_in(streams_of[2], 1), 0, 8).astype(jnp.int32)
    target = gaussian(streams_of[3], (NX, NY, VARS), 1.0, 6.0, ((0, 8), (1, 8)))
    w_self = gaussian(streams_of[4], (DEPTH_COUNT, D, D), D ** -0.5, 0.25)
    w_nbr = gaussian(streams_of[5], (DEPTH_COUNT, D, D), D ** -0.5, 0.25)
    w_out = gaussian(streams_of[6], (DEPTH_COUNT, D, D), D ** -0.5, 0.25)
    w_scale = gaussian(streams_of[7], (DEPTH_COUNT, NOISE, D), 0.1, 0.5, (), jnp.float32)
    w_shift = gaussian(streams_of[8], (DEPTH_COUNT, NOISE, D), 0.1, 0.5, (), jnp.float32)
    w_dec = gaussian(streams_of[9], (D, VARS), D ** -0.5, 0.25)
    return {"states": states, "noises": noises, "codes": codes, "target": target, "w_self": w_self, "w_nbr": w_nbr, "w_out": w_out, "w_scale": w_scale, "w_shift": w_shift, "w_dec": w_dec}


def norm_rows(x):
    mean = lax.optimization_barrier(jnp.mean(x, axis=-1, keepdims=True))
    var = lax.optimization_barrier(jnp.mean((x - mean) ** 2, axis=-1, keepdims=True))
    return (x - mean) / jnp.sqrt(var + 1e-05)

def aggregate(normed, codes):
    padded = jnp.pad(normed, ((1, 1), (1, 1), (0, 0)))
    line_indices_eastward, line_indices_northward = (normed.shape[0], normed.shape[1])
    total = jnp.zeros(normed.shape, jnp.float32)
    for code in range(9):
        displacement_east, displacement_north = (code // 3, code % 3)
        view = padded[displacement_east:displacement_east + line_indices_eastward, displacement_north:displacement_north + line_indices_northward]
        count = lax.optimization_barrier(jnp.sum((codes == code).astype(jnp.float32), axis=-1, keepdims=True))
        total = total + count * view.astype(jnp.float32)
    return (total / DEGREE).astype(jnp.bfloat16)

def run_member(state, noise, codes, w_self, w_nbr, w_out, w_scale, w_shift, w_dec):
    x = state.astype(jnp.float32)
    rows = x.shape[0] * x.shape[1]
    for layer in range(DEPTH_COUNT):
        scale = jnp.dot(noise, w_scale[layer], precision=lax.Precision.HIGHEST)
        shift = jnp.dot(noise, w_shift[layer], precision=lax.Precision.HIGHEST)
        normed = (norm_rows(x) * (1.0 + scale) + shift).astype(jnp.bfloat16)
        mixed = aggregate(normed, codes)
        pre = jnp.dot(normed.reshape(rows, -1), w_self[layer], preferred_element_type=jnp.float32)
        pre = pre + jnp.dot(mixed.reshape(rows, -1), w_nbr[layer], preferred_element_type=jnp.float32)
        hidden = jax.nn.silu(pre).astype(jnp.bfloat16)
        x = x + jnp.dot(hidden, w_out[layer], preferred_element_type=jnp.float32).reshape(x.shape)
    final = norm_rows(x).astype(jnp.bfloat16).reshape(rows, -1)
    out = jnp.dot(final, w_dec, preferred_element_type=jnp.float32).astype(jnp.bfloat16)
    return out.reshape(x.shape[0], x.shape[1], -1)

def reference(states, noises, codes, target, w_self, w_nbr, w_out, w_scale, w_shift, w_dec):

    def one(index):
        return run_member(states[index], noises[index], codes, w_self, w_nbr, w_out, w_scale, w_shift, w_dec)
    preds = lax.map(one, jnp.arange(MEMBERS))
    truth = target.astype(jnp.float32)
    skill = jnp.zeros(truth.shape, jnp.float32)
    spread = jnp.zeros(truth.shape, jnp.float32)
    for first in range(MEMBERS):
        value = preds[first].astype(jnp.float32)
        skill = skill + jnp.abs(value - truth)
        for second in range(MEMBERS):
            spread = spread + jnp.abs(value - preds[second].astype(jnp.float32))
    ranked_probability_score = skill / MEMBERS - spread / (2.0 * MEMBERS * (MEMBERS - 1))
    return (preds, ranked_probability_score)
```

```python
import jax
import jax.numpy as jnp
from jax import lax
from jax.sharding import PartitionSpec as P


def padded_2(shard, sides, width):
    for axis, dim in sides:
        peers, length = (lax.axis_size(axis), shard.shape[dim])
        up = [(i, (i + 1) % peers) for i in range(peers - 1)]
        down = [(j, i) for i, j in up]
        last = lax.slice_in_dim(shard, length - width, length, axis=dim)
        initial = lax.slice_in_dim(shard, 0, width, axis=dim)
        before = lax.ppermute(last, axis, up)
        after = lax.ppermute(initial, axis, down)
        shard = jnp.concatenate([before, shard, after], axis=dim)
    return shard


def norm_rows(x):
    mean = jnp.mean(x, axis=-1, keepdims=True)
    var = jnp.mean((x - mean) ** 2, axis=-1, keepdims=True)
    return (x - mean) / jnp.sqrt(var + 1e-05)


def local(states, noises, codes, target, w_self, w_nbr, w_out, w_scale, w_shift, w_dec):
    x = states[0].astype(jnp.float32)
    noise = noises[0]
    line_indices_eastward, line_indices_northward = (x.shape[0], x.shape[1])
    rows = line_indices_eastward * line_indices_northward
    degree = codes.shape[2]
    counts = [
        jnp.sum((codes == code).astype(jnp.float32), axis=-1, keepdims=True) for code in range(9)
    ]
    for layer in range(w_self.shape[0]):
        scale = jnp.dot(noise, w_scale[layer], precision=lax.Precision.HIGHEST)
        shift = jnp.dot(noise, w_shift[layer], precision=lax.Precision.HIGHEST)
        normed = (norm_rows(x) * (1.0 + scale) + shift).astype(jnp.bfloat16)
        padded = padded_2(normed, (("sx", 0), ("sy", 1)), 1)
        total = jnp.zeros(normed.shape, jnp.float32)
        for code in range(9):
            displacement_east, displacement_north = (code // 3, code % 3)
            view = padded[
                displacement_east : displacement_east + line_indices_eastward,
                displacement_north : displacement_north + line_indices_northward,
            ]
            total = total + counts[code] * view.astype(jnp.float32)
        mixed = (total / degree).astype(jnp.bfloat16)
        pre = jnp.dot(normed.reshape(rows, -1), w_self[layer], preferred_element_type=jnp.float32)
        pre = pre + jnp.dot(
            mixed.reshape(rows, -1), w_nbr[layer], preferred_element_type=jnp.float32
        )
        hidden = jax.nn.silu(pre).astype(jnp.bfloat16)
        x = x + jnp.dot(hidden, w_out[layer], preferred_element_type=jnp.float32).reshape(x.shape)
    final = norm_rows(x).astype(jnp.bfloat16).reshape(rows, -1)
    raveled_outputs = jnp.dot(final, w_dec, preferred_element_type=jnp.float32).astype(jnp.bfloat16)
    predicted_grid = raveled_outputs.reshape(1, line_indices_eastward, line_indices_northward, -1)
    truth = target.astype(jnp.float32)
    ensemble_entries = lax.axis_size("member")
    denom = 2.0 * ensemble_entries * (ensemble_entries - 1)
    variables = raveled_outputs.shape[-1]
    share = rows // ensemble_entries
    member = lax.axis_index("member")
    mine = lax.all_to_all(
        raveled_outputs.reshape(ensemble_entries, share, variables), "member", 0, 0
    ).astype(jnp.float32)
    truth = lax.dynamic_slice_in_dim(truth.reshape(rows, variables), member * share, share, 0)
    skill = jnp.zeros(truth.shape, jnp.float32)
    spread = jnp.zeros(truth.shape, jnp.float32)
    for first in range(ensemble_entries):
        skill = skill + jnp.abs(mine[first] - truth)
        for second in range(first):
            spread = spread + jnp.abs(mine[first] - mine[second])
    score = (skill / ensemble_entries - 2.0 * spread / denom).astype(jnp.bfloat16)
    copies = jnp.broadcast_to(score[None], (ensemble_entries,) + score.shape)
    scores = lax.all_to_all(copies, "member", 0, 0)
    ranked_probability_score = scores.astype(jnp.float32).reshape(target.shape)
    return (predicted_grid, ranked_probability_score)


def solution(mesh):
    placed = (
        P("member", "sx", "sy", None),
        P("member", None),
        P("sx", "sy", None),
        P("sx", "sy", None),
        P(),
        P(),
        P(),
        P(),
        P(),
        P(),
    )
    return jax.shard_map(
        local,
        mesh=mesh,
        in_specs=placed,
        out_specs=(P("member", "sx", "sy", None), P("sx", "sy", None)),
        check_vma=False,
    )
```

```python
import functools

import jax
import jax.numpy as jnp
from jax import lax
from jax.experimental import pallas as pl
from jax.experimental.pallas import tpu as pltpu
from jax.sharding import PartitionSpec as P

EAST = 32
NORTH = 16
OWN = EAST * NORTH
LONG = EAST + 4
PAD = 48
CODED = 40
FAR = 56
SIDE = 96
LANES = 128
OUT = OWN + 2 * NORTH + 2 * PAD
ALL = OUT + 2 * NORTH + 2 * PAD
EPS = 1e-05


def place(row, column):
    inner = jnp.where(
        (row >= 0) & (row < EAST),
        row * NORTH + column,
        jnp.where(
            row == -1,
            OWN + column,
            jnp.where(
                row == EAST,
                OWN + NORTH + column,
                jnp.where(row == -2, OUT + column, OUT + NORTH + column),
            ),
        ),
    )
    side = jnp.where(
        column == -1,
        OWN + 2 * NORTH,
        jnp.where(
            column == NORTH,
            OWN + 2 * NORTH + PAD,
            jnp.where(column == -2, OUT + 2 * NORTH, OUT + 2 * NORTH + PAD),
        ),
    )
    return jnp.where((column >= 0) & (column < NORTH), inner, side + row + 2)


def neighbours(codes, row, column, spot, sizes):
    third = (codes >= 3).astype(jnp.int32) + (codes >= 6).astype(jnp.int32)
    to_row = row + third - 1
    to_column = column + (codes - 3 * third) - 1
    east = spot[0] * EAST + to_row
    north = spot[1] * NORTH + to_column
    real = (east >= 0) & (east < sizes[0]) & (north >= 0) & (north < sizes[1])
    real = real & (row >= -1) & (row <= EAST)
    return jnp.where(real, place(to_row, to_column), -1)


def counted(index, width, degree):
    lanes = lax.broadcasted_iota(jnp.int32, (index.shape[0], width), 1)
    total = jnp.zeros(lanes.shape, jnp.float32)
    for slot in range(degree):
        total = total + jnp.where(lanes == index[:, slot : slot + 1], 1.0, 0.0)
    return total.astype(jnp.bfloat16)


def norm(x):
    away = x - jnp.mean(x, axis=-1, keepdims=True)
    var = jnp.mean(away * away, axis=-1, keepdims=True)
    return away * lax.rsqrt(var + EPS)


def dot(a, b):
    return jnp.dot(a, b, preferred_element_type=jnp.float32)


def rows_out(degree, top, bottom, codes, initial, last):
    for out, nodes, row in ((initial, top, 0), (last, bottom, EAST - 1)):
        lane = lax.broadcasted_iota(jnp.int32, (NORTH, LANES), 1)
        held = jnp.zeros((NORTH, LANES), jnp.int32)
        for slot in range(degree):
            held = jnp.where(lane == slot, codes[slot, :, row : row + 1], held)
        out[: 2 * NORTH] = nodes[...]
        out[2 * NORTH :] = jnp.zeros((NORTH, out.shape[1]), jnp.bfloat16)
        out[2 * NORTH :, :LANES] = held.astype(jnp.float32).astype(jnp.bfloat16)


def prepare(
    sizes, degree, spot, x, codes, noise, w_scale, w_shift, first, links, gains, sides, named
):
    for layer in range(w_scale.shape[0]):
        scale = jnp.sum(noise[...] * w_scale[layer], axis=0, keepdims=True)
        shift = jnp.sum(noise[...] * w_shift[layer], axis=0, keepdims=True)
        gains[2 * layer : 2 * layer + 1] = 1.0 + scale
        gains[2 * layer + 1 : 2 * layer + 2] = shift
    sides[...] = jnp.zeros(sides.shape, jnp.float32)
    named[...] = jnp.zeros(named.shape, jnp.float32)
    lines = 8
    rows = lines * NORTH
    for part in range(EAST // lines):
        here = slice(part * rows, (part + 1) * rows)
        state = x[here].astype(jnp.float32)
        held = codes[here]
        grid = state.reshape(lines, NORTH, state.shape[1])
        coded = held.astype(jnp.float32).reshape(lines, NORTH, degree)
        at = 2 + part * lines
        for side, (near, far) in enumerate(((0, 1), (NORTH - 1, NORTH - 2))):
            sides[side, at : at + lines] = grid[:, near]
            sides[side, FAR + at : FAR + at + lines] = grid[:, far]
            named[side, at : at + lines, :degree] = coded[:, near]
        first[here] = (norm(state) * gains[0:1] + gains[1:2]).astype(jnp.bfloat16)
        node = lax.broadcasted_iota(jnp.int32, (rows, degree), 0) + part * rows
        index = neighbours(held, node // NORTH, node % NORTH, (spot[0], spot[1]), sizes)
        links[here] = counted(index, OUT, degree)
    for side in range(2):
        for part in range(PAD // 16):
            sides[side, CODED:FAR, part * LANES : (part + 1) * LANES] = named[
                side, part * 16 : (part + 1) * 16
            ]


def columns_out(sides, before, after, initial, last, lines):
    top, bottom = (before[...].astype(jnp.float32), after[...].astype(jnp.float32))
    for side, (out, near, far) in enumerate(
        ((initial, 0, 1), (last, NORTH - 1, NORTH - 2))
    ):
        lines[...] = sides[side]
        for at, column in ((0, near), (FAR, far)):
            for step, source, row in (
                (0, top, 0), (1, top, 1), (EAST + 2, bottom, 0), (EAST + 3, bottom, 1)
            ):
                picked = row * NORTH + column
                lines[at + step : at + step + 1] = source[picked : picked + 1]
        picked = 2 * NORTH + near
        lines[CODED + 1 : CODED + 2, :LANES] = top[picked : picked + 1, :LANES]
        part, line = divmod(EAST + 2, 16)
        lines[CODED + line : CODED + line + 1, part * LANES : (part + 1) * LANES] = bottom[
            picked : picked + 1, :LANES
        ]
        out[...] = lines[...].astype(jnp.bfloat16)


def advance(
    sizes, degree, spot, x, first, links, gains, before, after, left, right,
    w_self, w_nbr, w_out, w_dec, preds, a, g, state,
):
    place_here = (spot[0], spot[1])
    gain, offset = gains[0:1], gains[1:2]

    def active(v):
        return (norm(v.astype(jnp.float32)) * gain + offset).astype(jnp.bfloat16)

    top, bottom, west, east = (
        arrived[...].astype(jnp.float32) for arrived in (before, after, left, right)
    )
    state[0:OWN] = x[...].astype(jnp.float32)
    at = OWN
    for ring_part in (top[NORTH : 2 * NORTH], bottom[:NORTH], west[:PAD], east[:PAD]):
        state[at : at + ring_part.shape[0]] = ring_part
        at += ring_part.shape[0]
    a[0:OWN] = first[...]
    a[OWN:OUT] = active(state[OWN:OUT])
    gap = jnp.zeros((PAD - SIDE + FAR, west.shape[1]), jnp.float32)
    second = [top[:NORTH], bottom[NORTH : 2 * NORTH], west[FAR:], gap, east[FAR:], gap]
    a[OUT:] = active(jnp.concatenate(second, axis=0))

    ring = []
    for arrived, row0, column0 in ((top, -1, 0), (bottom, EAST, 0), (west, -2, -1), (east, -2, NORTH)):
        if column0 == 0:
            held = arrived[2 * NORTH : 3 * NORTH, :LANES]
        else:
            held = jnp.concatenate(
                [arrived[CODED:FAR, i * LANES : (i + 1) * LANES] for i in range(PAD // 16)], axis=0
            )
        held = held[:, :degree].astype(jnp.int32)
        step = lax.broadcasted_iota(jnp.int32, held.shape, 0)
        if column0 == 0:
            row, column = (jnp.full(held.shape, row0, jnp.int32), step)
        else:
            row, column = (row0 + step, jnp.full(held.shape, column0, jnp.int32))
        index = neighbours(held, row, column, place_here, sizes)
        ring.append(counted(index, ALL, degree))
    ring = jnp.concatenate(ring, axis=0)

    sixth = 1.0 / degree
    g[0:OWN] = (dot(links[...], a[0:OUT]) * sixth).astype(jnp.bfloat16)
    g[OWN:OUT] = (dot(ring, a[...]) * sixth).astype(jnp.bfloat16)
    pre = dot(a[0:OUT], w_self[0]) + dot(g[...], w_nbr[0])
    hidden = jax.nn.silu(pre).astype(jnp.bfloat16)
    state[...] = state[...] + dot(hidden, w_out[0])

    gain, offset = gains[2:3], gains[3:4]
    a[0:OUT] = active(state[...])
    g[0:OWN] = (dot(links[...], a[0:OUT]) * sixth).astype(jnp.bfloat16)
    pre = dot(a[0:OWN], w_self[1]) + dot(g[0:OWN], w_nbr[1])
    hidden = jax.nn.silu(pre).astype(jnp.bfloat16)
    final = norm(state[0:OWN] + dot(hidden, w_out[1])).astype(jnp.bfloat16)
    preds[...] = dot(final, w_dec[...]).astype(jnp.bfloat16)


def score_share(mine, truth, copies):
    members = mine.shape[0]
    denom = 2.0 * members * (members - 1)
    held = [mine[one].astype(jnp.float32) for one in range(members)]
    goal = truth[...].astype(jnp.float32)
    skill = jnp.zeros(goal.shape, jnp.float32)
    spread = jnp.zeros(goal.shape, jnp.float32)
    for one in range(members):
        skill = skill + jnp.abs(held[one] - goal)
        for two in range(one):
            spread = spread + jnp.abs(held[one] - held[two])
    score = (skill * (1.0 / members) - spread * (2.0 / denom)).astype(jnp.bfloat16)
    for one in range(members):
        copies[one] = score


def swap(last, initial, axis):
    peers = lax.axis_size(axis)
    up = [(i, i + 1) for i in range(peers - 1)]
    down = [(j, i) for i, j in up]
    return lax.ppermute(last, axis, up), lax.ppermute(initial, axis, down)


def local(states, noises, codes, target, w_self, w_nbr, w_out, w_scale, w_shift, w_dec):
    width = states.shape[-1]
    degree = codes.shape[-1]
    variables = w_dec.shape[-1]
    layers = w_self.shape[0]
    x = states.reshape(OWN, width)
    sizes = (lax.axis_size("sx") * EAST, lax.axis_size("sy") * NORTH)
    spot = jnp.stack([lax.axis_index("sx"), lax.axis_index("sy")]).astype(jnp.int32)
    smem = pl.BlockSpec(memory_space=pltpu.SMEM)
    vmem = pl.BlockSpec(memory_space=pltpu.VMEM)

    def like(shape, dtype=jnp.bfloat16):
        return jax.ShapeDtypeStruct(shape, dtype)

    def limits(mib):
        return pltpu.CompilerParams(vmem_limit_bytes=mib << 20)

    def cost(flops, size):
        return pl.CostEstimate(flops=flops, bytes_accessed=size, transcendentals=0)

    initial, last = pl.pallas_call(
        functools.partial(rows_out, degree),
        grid=(1,),
        out_shape=(like((3 * NORTH, width)),) * 2,
        in_specs=[
            pl.BlockSpec((2 * NORTH, width), lambda i: (0, 0)),
            pl.BlockSpec((2 * NORTH, width), lambda i: (OWN // (2 * NORTH) - 1, 0)),
            pl.BlockSpec((degree, NORTH, EAST), lambda i: (0, 0, 0)),
        ],
        out_specs=(pl.BlockSpec((3 * NORTH, width), lambda i: (0, 0)),) * 2,
        compiler_params=limits(8),
        name="rows_out",
    )(x, x, codes.transpose(2, 1, 0))
    before, after = swap(last, initial, "sx")

    first, links, gains, sides = pl.pallas_call(
        functools.partial(prepare, sizes, degree),
        out_shape=(
            like((OWN, width)),
            like((OWN, OUT)),
            like((2 * layers, width), jnp.float32),
            like((2, SIDE, width), jnp.float32),
        ),
        in_specs=[smem] + [vmem] * 5,
        out_specs=(vmem,) * 4,
        scratch_shapes=[pltpu.VMEM((2, PAD, LANES), jnp.float32)],
        compiler_params=limits(16),
        cost_estimate=cost(1 << 24, 1 << 21),
        name="prepare",
    )(spot, x, codes.reshape(OWN, degree), noises.reshape(-1, 1), w_scale, w_shift)

    initial, last = pl.pallas_call(
        columns_out,
        out_shape=(like((SIDE, width)),) * 2,
        in_specs=[vmem] * 3,
        out_specs=(vmem,) * 2,
        scratch_shapes=[pltpu.VMEM((SIDE, width), jnp.float32)],
        compiler_params=limits(8),
        name="columns_out",
    )(sides, before, after)
    left, right = swap(last, initial, "sy")

    preds = pl.pallas_call(
        functools.partial(advance, sizes, degree),
        out_shape=like((OWN, variables)),
        in_specs=[smem] + [vmem] * 12,
        out_specs=vmem,
        scratch_shapes=[
            pltpu.VMEM((ALL, width), jnp.bfloat16),
            pltpu.VMEM((OUT, width), jnp.bfloat16),
            pltpu.VMEM((OUT, width), jnp.float32),
        ],
        compiler_params=limits(32),
        cost_estimate=cost(1 << 31, 1 << 23),
        name="advance",
    )(spot, x, first, links, gains, before, after, left, right, w_self, w_nbr, w_out, w_dec)

    members = lax.axis_size("member")
    share = OWN // members
    mine = lax.all_to_all(preds.reshape(members, share, variables), "member", 0, 0)
    truth = lax.dynamic_slice_in_dim(
        target.reshape(OWN, variables), lax.axis_index("member") * share, share, 0
    )
    copies = pl.pallas_call(
        score_share,
        out_shape=like(mine.shape),
        in_specs=[vmem] * 2,
        out_specs=vmem,
        compiler_params=limits(8),
        name="score_share",
    )(mine, truth)
    scores = lax.all_to_all(copies, "member", 0, 0).astype(jnp.float32)
    return (preds.reshape(1, EAST, NORTH, variables), scores.reshape(target.shape))


def solution(mesh):
    placed = (
        P("member", "sx", "sy", None),
        P("member", None),
        P("sx", "sy", None),
        P("sx", "sy", None),
        P(),
        P(),
        P(),
        P(),
        P(),
        P(),
    )
    return jax.shard_map(
        local,
        mesh=mesh,
        in_specs=placed,
        out_specs=(P("member", "sx", "sy", None), P("sx", "sy", None)),
        check_vma=False,
    )
```

```python
import functools

import jax
import jax.numpy as jnp
from jax import lax
from jax.experimental import pallas as pl
from jax.experimental.pallas import tpu as pltpu
from jax.sharding import PartitionSpec as P

EAST = 32
NORTH = 16
OWN = EAST * NORTH
LONG = EAST + 4
PAD = 48
CODED = 40
FAR = 56
SIDE = 96
LANES = 128
CODE = 1024
OUT = OWN + 2 * NORTH + 2 * PAD
ALL = OUT + 2 * NORTH + 2 * PAD
EPS = 1e-05


def place(row, column):
    inner = jnp.where(
        (row >= 0) & (row < EAST),
        row * NORTH + column,
        jnp.where(
            row == -1,
            OWN + column,
            jnp.where(
                row == EAST,
                OWN + NORTH + column,
                jnp.where(row == -2, OUT + column, OUT + NORTH + column),
            ),
        ),
    )
    side = jnp.where(
        column == -1,
        OWN + 2 * NORTH,
        jnp.where(
            column == NORTH,
            OWN + 2 * NORTH + PAD,
            jnp.where(column == -2, OUT + 2 * NORTH, OUT + 2 * NORTH + PAD),
        ),
    )
    return jnp.where((column >= 0) & (column < NORTH), inner, side + row + 2)


def neighbours(codes, row, column, spot, sizes):
    third = (codes >= 3).astype(jnp.int32) + (codes >= 6).astype(jnp.int32)
    to_row = row + third - 1
    to_column = column + (codes - 3 * third) - 1
    east = spot[0] * EAST + to_row
    north = spot[1] * NORTH + to_column
    real = (east >= 0) & (east < sizes[0]) & (north >= 0) & (north < sizes[1])
    real = real & (row >= -1) & (row <= EAST)
    return jnp.where(real, place(to_row, to_column), -1)


def counted(index, at, width, degree):
    lanes = lax.broadcasted_iota(jnp.int32, (index.shape[0], width), 1) + at
    total = jnp.zeros(lanes.shape, jnp.float32)
    for slot in range(degree):
        total = total + jnp.where(lanes == index[:, slot : slot + 1], 1.0, 0.0)
    return total.astype(jnp.bfloat16)


def norm(x):
    away = x - jnp.mean(x, axis=-1, keepdims=True)
    var = jnp.mean(away * away, axis=-1, keepdims=True)
    return away * lax.rsqrt(var + EPS)


def dot(a, b):
    return jnp.dot(a, b, preferred_element_type=jnp.float32)


def here(axis):
    return lax.axis_index(axis).astype(jnp.int32)


def rows_out(degree, top, bottom, codes, far_out, near_out):
    lane = lax.broadcasted_iota(jnp.int32, (NORTH, LANES), 1)
    lines = []
    for row in (0, EAST - 1):
        named = jnp.zeros((NORTH, LANES), jnp.int32)
        for slot in range(degree):
            named = jnp.where(lane == slot, codes[slot, :, row : row + 1], named)
        lines.append(named.astype(jnp.float32).astype(jnp.bfloat16))
    odd = here("sx") % 2 == 1
    for out, is_top in ((far_out, jnp.logical_not(odd)), (near_out, odd)):
        out[: 2 * NORTH] = jnp.where(is_top, top[...], bottom[...])
        out[2 * NORTH :] = jnp.zeros((NORTH, out.shape[1]), jnp.bfloat16)
        out[2 * NORTH :, :LANES] = jnp.where(is_top, lines[0], lines[1])


def sorted_by(axis, far, near):
    odd = here(axis) % 2 == 1
    far, near = (far[...].astype(jnp.float32), near[...].astype(jnp.float32))
    return jnp.where(odd, near, far), jnp.where(odd, far, near)


def collect(degree, x, coded, sides, named):
    sides[...] = jnp.zeros(sides.shape, jnp.float32)
    named[...] = jnp.zeros(named.shape, jnp.float32)
    lines = 8
    rows = lines * NORTH
    for part in range(EAST // lines):
        span = slice(part * rows, (part + 1) * rows)
        grid = x[span].astype(jnp.float32).reshape(lines, NORTH, x.shape[1])
        held = coded[span].reshape(lines, NORTH, degree)
        at = 2 + part * lines
        for side, (near, far) in enumerate(((0, 1), (NORTH - 1, NORTH - 2))):
            sides[side, at : at + lines] = grid[:, near]
            sides[side, FAR + at : FAR + at + lines] = grid[:, far]
            named[side, at : at + lines, :degree] = (held[:, near] >> 10).astype(jnp.float32)
    for side in range(2):
        for part in range(PAD // 16):
            sides[side, CODED:FAR, part * LANES : (part + 1) * LANES] = named[
                side, part * 16 : (part + 1) * 16
            ]


def prepare(
    degree, x, coded, noise, w_scale, w_shift, w_self, sent,
    first, links, gains, own_sum, own_part,
):
    for layer in range(w_scale.shape[0]):
        for at, w in enumerate((w_scale, w_shift)):
            gains[2 * layer + at : 2 * layer + at + 1] = (1.0 - at) + jnp.dot(
                noise[...], w[layer], precision=lax.Precision.HIGHEST,
                preferred_element_type=jnp.float32,
            )
    links[...] = jnp.zeros(links.shape, jnp.bfloat16)
    rows = OWN // 4
    for part in range(4):
        span = slice(part * rows, (part + 1) * rows)
        state = x[span].astype(jnp.float32)
        first[span] = (norm(state) * gains[0:1] + gains[1:2]).astype(jnp.bfloat16)
    for row in range(EAST):
        span = slice(row * NORTH, (row + 1) * NORTH)
        index = (coded[span] & (CODE - 1)) - 1
        tiles = {max(row - 1, 0) * NORTH // LANES, min(row + 1, EAST - 1) * NORTH // LANES}
        for tile in sorted(tiles) + [OWN // LANES]:
            links[span, tile * LANES : (tile + 1) * LANES] = counted(
                index, tile * LANES, LANES, degree
            )
    for part in range(2):
        span = slice(part * OWN // 2, (part + 1) * OWN // 2)
        own_part[span] = dot(first[span], w_self[0])
        own_sum[span] = dot(links[span, :OWN], first[...])


def columns_out(sides, far_row, near_row, far_out, near_out, lines):
    top, bottom = sorted_by("sx", far_row, near_row)
    for side, (near, far) in enumerate(((0, 1), (NORTH - 1, NORTH - 2))):
        lines[side] = sides[side]
        for at, column in ((0, near), (FAR, far)):
            for step, source, row in (
                (0, top, 0), (1, top, 1), (EAST + 2, bottom, 0), (EAST + 3, bottom, 1)
            ):
                picked = row * NORTH + column
                lines[side, at + step : at + step + 1] = source[picked : picked + 1]
        picked = 2 * NORTH + near
        lines[side, CODED + 1 : CODED + 2, :LANES] = top[picked : picked + 1, :LANES]
        part, line = divmod(EAST + 2, 16)
        lines[side, CODED + line : CODED + line + 1, part * LANES : (part + 1) * LANES] = bottom[
            picked : picked + 1, :LANES
        ]
    odd = here("sy") % 2
    far_out[...] = lines[odd].astype(jnp.bfloat16)
    near_out[...] = lines[1 - odd].astype(jnp.bfloat16)


def advance(
    sizes, degree, x, links, gains, own_sum, own_part, far_row, near_row, far_column, near_column,
    w_self, w_nbr, w_out, w_dec, first, preds, sent, rim_first, second, total, part, rim, ring,
):
    place_here = (here("sx"), here("sy"))
    sixth = 1.0 / degree

    def active(v, layer):
        return (norm(v) * gains[2 * layer : 2 * layer + 1] + gains[2 * layer + 1 : 2 * layer + 2]).astype(
            jnp.bfloat16
        )

    top, bottom = sorted_by("sx", far_row, near_row)
    west, east = sorted_by("sy", far_column, near_column)
    gap = jnp.zeros((PAD - SIDE + FAR, west.shape[1]), jnp.float32)
    rims = (
        (top[NORTH : 2 * NORTH], bottom[:NORTH], west[:PAD], east[:PAD]),
        (top[:NORTH], bottom[NORTH : 2 * NORTH], west[FAR:], gap, east[FAR:], gap),
    )
    at = 0
    for ring_parts in rims:
        for nodes in ring_parts:
            rim[at : at + nodes.shape[0]] = nodes
            at += nodes.shape[0]

    at = 0
    for arrived, row0, column0 in ((top, -1, 0), (bottom, EAST, 0), (west, -2, -1), (east, -2, NORTH)):
        if column0 == 0:
            held = arrived[2 * NORTH : 3 * NORTH, :LANES]
        else:
            held = jnp.concatenate(
                [arrived[CODED:FAR, i * LANES : (i + 1) * LANES] for i in range(PAD // 16)], axis=0
            )
        held = held[:, :degree].astype(jnp.int32)
        step = lax.broadcasted_iota(jnp.int32, held.shape, 0)
        if column0 == 0:
            row, column = (jnp.full(held.shape, row0, jnp.int32), step)
        else:
            row, column = (row0 + step, jnp.full(held.shape, column0, jnp.int32))
        index = neighbours(held, row, column, place_here, sizes)
        ring[at : at + held.shape[0]] = counted(index, 0, ALL, degree)
        at += held.shape[0]

    def rest(total, part, layer):
        hidden = jax.nn.silu(part + dot(total, w_nbr[layer])).astype(jnp.bfloat16)
        return dot(hidden, w_out[layer])

    rim_first[...] = active(rim[...], 0)
    near = slice(0, OUT - OWN)
    own = slice(0, OWN)
    total[own] = ((own_sum[...] + dot(links[:, OWN:], rim_first[near])) * sixth).astype(jnp.bfloat16)
    total[OWN:] = (
        (dot(ring[:, :OWN], first[...]) + dot(ring[:, OWN:], rim_first[...])) * sixth
    ).astype(jnp.bfloat16)
    part[own] = own_part[...]
    part[OWN:] = dot(rim_first[near], w_self[0])
    v = rest(total[...], part[...], 0)
    part[own] = x[...].astype(jnp.float32) + v[own]
    part[OWN:] = rim[near] + v[OWN:]
    second[...] = active(part[...], 1)
    total[own] = (dot(links[...], second[...]) * sixth).astype(jnp.bfloat16)
    v = part[own] + rest(total[own], dot(second[own], w_self[1]), 1)
    value = dot(norm(v).astype(jnp.bfloat16), w_dec[...]).astype(jnp.bfloat16)
    preds[...] = value
    sent[...] = value


def score_share(mine, truth, copies):
    members, share, _ = mine.shape
    denom = 2.0 * members * (members - 1)
    held = [mine[one].astype(jnp.float32) for one in range(members)]
    goal = truth[pl.ds(pl.multiple_of(here("member") * share, share), share)].astype(jnp.float32)
    skill = jnp.zeros(goal.shape, jnp.float32)
    spread = jnp.zeros(goal.shape, jnp.float32)
    for one in range(members):
        skill = skill + jnp.abs(held[one] - goal)
        for two in range(one):
            spread = spread + jnp.abs(held[one] - held[two])
    score = (skill * (1.0 / members) - spread * (2.0 / denom)).astype(jnp.bfloat16)
    for one in range(members):
        copies[one] = score


def swap(far, near, axis):
    peers = lax.axis_size(axis)
    pairs = [[(i, i + 1), (i + 1, i)] for i in range(peers - 1)]
    return (
        lax.ppermute(far, axis, sum(pairs[1::2], [])),
        lax.ppermute(near, axis, sum(pairs[0::2], [])),
    )


def local(states, noises, codes, target, w_self, w_nbr, w_out, w_scale, w_shift, w_dec):
    width = states.shape[-1]
    degree = codes.shape[-1]
    variables = w_dec.shape[-1]
    layers = w_self.shape[0]
    x = states.reshape(OWN, width)
    sizes = (lax.axis_size("sx") * EAST, lax.axis_size("sy") * NORTH)
    vmem = pl.BlockSpec(memory_space=pltpu.VMEM)

    def like(shape, dtype=jnp.bfloat16):
        return jax.ShapeDtypeStruct(shape, dtype)

    def limits(mib):
        return pltpu.CompilerParams(vmem_limit_bytes=mib << 20)

    def cost(flops, size):
        return pl.CostEstimate(flops=flops, bytes_accessed=size, transcendentals=0)

    slots = codes.transpose(2, 1, 0)
    far_row, near_row = swap(
        *pl.pallas_call(
            functools.partial(rows_out, degree),
            grid=(1,),
            out_shape=(like((3 * NORTH, width)),) * 2,
            in_specs=[
                pl.BlockSpec((2 * NORTH, width), lambda i: (0, 0)),
                pl.BlockSpec((2 * NORTH, width), lambda i: (OWN // (2 * NORTH) - 1, 0)),
                pl.BlockSpec(slots.shape, lambda i: (0, 0, 0)),
            ],
            out_specs=(pl.BlockSpec((3 * NORTH, width), lambda i: (0, 0)),) * 2,
            compiler_params=limits(60),
            name="rows_out",
        )(x, x, slots),
        "sx",
    )

    index = neighbours(
        slots,
        lax.broadcasted_iota(jnp.int32, slots.shape, 2),
        lax.broadcasted_iota(jnp.int32, slots.shape, 1),
        (here("sx"), here("sy")),
        sizes,
    )
    coded = (index + 1 + CODE * slots).transpose(2, 1, 0).reshape(OWN, degree)
    sides = pl.pallas_call(
        functools.partial(collect, degree),
        out_shape=like((2, SIDE, width), jnp.float32),
        in_specs=[vmem] * 2,
        out_specs=vmem,
        scratch_shapes=[pltpu.VMEM((2, PAD, LANES), jnp.float32)],
        compiler_params=limits(8),
        cost_estimate=cost(1 << 20, 1 << 24),
        name="collect",
    )(x, coded)

    sent = pl.pallas_call(
        columns_out,
        out_shape=(like((SIDE, width)),) * 2,
        in_specs=[vmem] * 3,
        out_specs=(vmem,) * 2,
        scratch_shapes=[pltpu.VMEM((2, SIDE, width), jnp.float32)],
        compiler_params=limits(8),
        name="columns_out",
    )(sides, far_row, near_row)
    far_column, near_column = swap(*sent, "sy")

    first, links, gains, own_sum, own_part = pl.pallas_call(
        functools.partial(prepare, degree),
        out_shape=(
            like((OWN, width)),
            like((OWN, OUT)),
            like((2 * layers, width), jnp.float32),
            like((OWN, width), jnp.float32),
            like((OWN, width), jnp.float32),
        ),
        in_specs=[vmem] * 6 + [pl.BlockSpec(memory_space=pl.ANY)],
        out_specs=(vmem,) * 5,
        compiler_params=limits(16),
        cost_estimate=cost(1 << 24, 1 << 25),
        name="prepare",
    )(x, coded, noises, w_scale, w_shift, w_self, sent[1])

    preds, shares = pl.pallas_call(
        functools.partial(advance, sizes, degree),
        out_shape=(like((OWN, variables)),) * 2,
        in_specs=[vmem] * 14,
        out_specs=(vmem,) * 2,
        scratch_shapes=[
            pltpu.VMEM((ALL - OWN, width), jnp.bfloat16),
            pltpu.VMEM((OUT, width), jnp.bfloat16),
            pltpu.VMEM((OUT, width), jnp.bfloat16),
            pltpu.VMEM((OUT, width), jnp.float32),
            pltpu.VMEM((ALL - OWN, width), jnp.float32),
            pltpu.VMEM((OUT - OWN, ALL), jnp.bfloat16),
        ],
        compiler_params=limits(16),
        cost_estimate=cost(1 << 31, 1 << 23),
        name="advance",
    )(
        x, links, gains, own_sum, own_part, far_row, near_row, far_column, near_column,
        w_self, w_nbr, w_out, w_dec, first,
    )

    members = lax.axis_size("member")
    share = OWN // members
    mine = lax.all_to_all(shares.reshape(members, share, variables), "member", 0, 0)
    copies = pl.pallas_call(
        score_share,
        out_shape=like(mine.shape),
        in_specs=[vmem] * 2,
        out_specs=vmem,
        compiler_params=limits(8),
        name="score_share",
    )(mine, target.reshape(OWN, variables))
    scores = lax.all_to_all(copies, "member", 0, 0).astype(jnp.float32)
    return (preds.reshape(1, EAST, NORTH, variables), scores.reshape(target.shape))


def solution(mesh):
    placed = (
        P("member", "sx", "sy", None),
        P("member", None),
        P("sx", "sy", None),
        P("sx", "sy", None),
        P(),
        P(),
        P(),
        P(),
        P(),
        P(),
    )
    return jax.shard_map(
        local,
        mesh=mesh,
        in_specs=placed,
        out_specs=(P("member", "sx", "sy", None), P("sx", "sy", None)),
        check_vma=False,
    )
```

```python
import functools

import jax
import jax.numpy as jnp
from jax import lax
from jax.experimental import pallas as pl
from jax.experimental.pallas import tpu as pltpu
from jax.sharding import PartitionSpec as P

EAST = 32
NORTH = 16
OWN = EAST * NORTH
LONG = EAST + 4
PAD = 48
CODED = 40
FAR = 56
SIDE = 96
LANES = 128
CODE = 1024
OUT = OWN + 2 * NORTH + 2 * PAD
ALL = OUT + 2 * NORTH + 2 * PAD
EPS = 1e-05


def place(row, column):
    inner = jnp.where(
        (row >= 0) & (row < EAST),
        row * NORTH + column,
        jnp.where(
            row == -1,
            OWN + column,
            jnp.where(
                row == EAST,
                OWN + NORTH + column,
                jnp.where(row == -2, OUT + column, OUT + NORTH + column),
            ),
        ),
    )
    side = jnp.where(
        column == -1,
        OWN + 2 * NORTH,
        jnp.where(
            column == NORTH,
            OWN + 2 * NORTH + PAD,
            jnp.where(column == -2, OUT + 2 * NORTH, OUT + 2 * NORTH + PAD),
        ),
    )
    return jnp.where((column >= 0) & (column < NORTH), inner, side + row + 2)


def neighbours(codes, row, column, spot, sizes):
    third = (codes >= 3).astype(jnp.int32) + (codes >= 6).astype(jnp.int32)
    to_row = row + third - 1
    to_column = column + (codes - 3 * third) - 1
    east = spot[0] * EAST + to_row
    north = spot[1] * NORTH + to_column
    real = (east >= 0) & (east < sizes[0]) & (north >= 0) & (north < sizes[1])
    real = real & (row >= -1) & (row <= EAST)
    return jnp.where(real, place(to_row, to_column), -1)


def counted(index, at, width, degree):
    lanes = lax.broadcasted_iota(jnp.int32, (index.shape[0], width), 1) + at
    total = jnp.zeros(lanes.shape, jnp.float32)
    for slot in range(degree):
        total = total + jnp.where(lanes == index[:, slot : slot + 1], 1.0, 0.0)
    return total.astype(jnp.bfloat16)


def norm(x):
    away = x - jnp.mean(x, axis=-1, keepdims=True)
    var = jnp.mean(away * away, axis=-1, keepdims=True)
    return away * lax.rsqrt(var + EPS)


def dot(a, b):
    return jnp.dot(a, b, preferred_element_type=jnp.float32)


def here(axis):
    return lax.axis_index(axis).astype(jnp.int32)


def rows_out(degree, top, bottom, codes, far_out, near_out):
    lane = lax.broadcasted_iota(jnp.int32, (NORTH, LANES), 1)
    lines = []
    for row in (0, EAST - 1):
        named = jnp.zeros((NORTH, LANES), jnp.int32)
        for slot in range(degree):
            named = jnp.where(lane == slot, codes[slot, :, row : row + 1], named)
        lines.append(named.astype(jnp.float32).astype(jnp.bfloat16))
    odd = here("sx") % 2 == 1
    for out, is_top in ((far_out, jnp.logical_not(odd)), (near_out, odd)):
        out[: 2 * NORTH] = jnp.where(is_top, top[...], bottom[...])
        out[2 * NORTH :] = jnp.zeros((NORTH, out.shape[1]), jnp.bfloat16)
        out[2 * NORTH :, :LANES] = jnp.where(is_top, lines[0], lines[1])


def sorted_by(axis, far, near):
    odd = here(axis) % 2 == 1
    far, near = (far[...].astype(jnp.float32), near[...].astype(jnp.float32))
    return jnp.where(odd, near, far), jnp.where(odd, far, near)


def collect(degree, x, coded, sides, named):
    sides[...] = jnp.zeros(sides.shape, jnp.float32)
    named[...] = jnp.zeros(named.shape, jnp.float32)
    lines = 8
    rows = lines * NORTH
    for part in range(EAST // lines):
        span = slice(part * rows, (part + 1) * rows)
        grid = x[span].astype(jnp.float32).reshape(lines, NORTH, x.shape[1])
        held = coded[span].reshape(lines, NORTH, degree)
        at = 2 + part * lines
        for side, (near, far) in enumerate(((0, 1), (NORTH - 1, NORTH - 2))):
            sides[side, at : at + lines] = grid[:, near]
            sides[side, FAR + at : FAR + at + lines] = grid[:, far]
            named[side, at : at + lines, :degree] = (held[:, near] >> 10).astype(jnp.float32)
    for side in range(2):
        for part in range(PAD // 16):
            sides[side, CODED:FAR, part * LANES : (part + 1) * LANES] = named[
                side, part * 16 : (part + 1) * 16
            ]


def active(v, gains, layer):
    return norm(v) * gains[2 * layer : 2 * layer + 1] + gains[2 * layer + 1 : 2 * layer + 2]


def rest(total, part, w_nbr, w_out, layer):
    hidden = jax.nn.silu(part + dot(total, w_nbr[layer])).astype(jnp.bfloat16)
    return dot(hidden, w_out[layer])


def ends(v):
    grid = v.reshape(EAST, NORTH, v.shape[-1])
    return jnp.concatenate([grid[:, 0], grid[:, NORTH - 1]], axis=0)


def split(out, v):
    for tile in range(out.shape[0]):
        out[tile] = v[:, tile * LANES : (tile + 1) * LANES]


def joined(tiles):
    return jnp.concatenate([tiles[tile] for tile in range(tiles.shape[0])], axis=1)


def prepare(
    degree, x, coded, noise, w_scale, w_shift, w_self, w_nbr, w_out, far_row, near_row, sent,
    first, links, gains, end_links, end_sum, end_part, x1, a1, own_sum, own_part, rim,
):
    for layer in range(w_scale.shape[0]):
        for at, w in enumerate((w_scale, w_shift)):
            gains[2 * layer + at : 2 * layer + at + 1] = (1.0 - at) + jnp.dot(
                noise[...], w[layer], precision=lax.Precision.HIGHEST,
                preferred_element_type=jnp.float32,
            )
    links[...] = jnp.zeros(links.shape, jnp.bfloat16)
    first[...] = active(x[...].astype(jnp.float32), gains, 0).astype(jnp.bfloat16)
    for row in range(EAST):
        span = slice(row * NORTH, (row + 1) * NORTH)
        index = (coded[span] & (CODE - 1)) - 1
        tiles = {max(row - 1, 0) * NORTH // LANES, min(row + 1, EAST - 1) * NORTH // LANES}
        for tile in sorted(tiles) + [OWN // LANES]:
            links[span, tile * LANES : (tile + 1) * LANES] = counted(
                index, tile * LANES, LANES, degree
            )
    end_links[...] = counted(ends((coded[...] & (CODE - 1)) - 1), OWN, OUT - OWN, degree)

    top, bottom = sorted_by("sx", far_row, near_row)
    rim[: 2 * NORTH] = active(
        jnp.concatenate([top[NORTH : 2 * NORTH], bottom[:NORTH]], axis=0), gains, 0
    ).astype(jnp.bfloat16)
    rim[2 * NORTH :] = jnp.zeros((rim.shape[0] - 2 * NORTH, rim.shape[1]), jnp.bfloat16)
    own_part[...] = dot(first[...], w_self[0])
    own_sum[...] = dot(links[:, :OWN], first[...])
    end_part[...] = ends(own_part[...])
    end_sum[...] = ends(own_sum[...])
    total = own_sum[...] + dot(links[:, OWN:], rim[...])
    total = (total * (1.0 / degree)).astype(jnp.bfloat16)
    v = x[...].astype(jnp.float32) + rest(total, own_part[...], w_nbr, w_out, 0)
    split(x1, v)
    split(a1, active(v, gains, 1))


def columns_out(w_out, sides, far_row, near_row, far_out, near_out, lines):
    top, bottom = sorted_by("sx", far_row, near_row)
    for side, (near, far) in enumerate(((0, 1), (NORTH - 1, NORTH - 2))):
        lines[side] = sides[side]
        for at, column in ((0, near), (FAR, far)):
            for step, source, row in (
                (0, top, 0), (1, top, 1), (EAST + 2, bottom, 0), (EAST + 3, bottom, 1)
            ):
                picked = row * NORTH + column
                lines[side, at + step : at + step + 1] = source[picked : picked + 1]
        picked = 2 * NORTH + near
        lines[side, CODED + 1 : CODED + 2, :LANES] = top[picked : picked + 1, :LANES]
        part, line = divmod(EAST + 2, 16)
        lines[side, CODED + line : CODED + line + 1, part * LANES : (part + 1) * LANES] = bottom[
            picked : picked + 1, :LANES
        ]
    odd = here("sy") % 2
    far_out[...] = lines[odd].astype(jnp.bfloat16)
    near_out[...] = lines[1 - odd].astype(jnp.bfloat16)


def advance(
    sizes, degree, first, links, gains, end_links, end_sum, end_part, old_x1, old_a1, sides,
    far_row, near_row, far_column, near_column, w_self, w_nbr, w_out, w_dec,
    preds, sent, x1, a1, rim_first, second, total, part, rim, ring,
):
    place_here = (here("sx"), here("sy"))
    sixth = 1.0 / degree

    top, bottom = sorted_by("sx", far_row, near_row)
    west, east = sorted_by("sy", far_column, near_column)
    gap = jnp.zeros((PAD - SIDE + FAR, west.shape[1]), jnp.float32)
    rims = (
        (top[NORTH : 2 * NORTH], bottom[:NORTH], west[:PAD], east[:PAD]),
        (top[:NORTH], bottom[NORTH : 2 * NORTH], west[FAR:], gap, east[FAR:], gap),
    )
    at = 0
    for ring_parts in rims:
        for nodes in ring_parts:
            rim[at : at + nodes.shape[0]] = nodes
            at += nodes.shape[0]

    at = 0
    for arrived, row0, column0 in ((top, -1, 0), (bottom, EAST, 0), (west, -2, -1), (east, -2, NORTH)):
        if column0 == 0:
            held = arrived[2 * NORTH : 3 * NORTH, :LANES]
        else:
            held = jnp.concatenate(
                [arrived[CODED:FAR, i * LANES : (i + 1) * LANES] for i in range(PAD // 16)], axis=0
            )
        held = held[:, :degree].astype(jnp.int32)
        step = lax.broadcasted_iota(jnp.int32, held.shape, 0)
        if column0 == 0:
            row, column = (jnp.full(held.shape, row0, jnp.int32), step)
        else:
            row, column = (row0 + step, jnp.full(held.shape, column0, jnp.int32))
        index = neighbours(held, row, column, place_here, sizes)
        ring[at : at + held.shape[0]] = counted(index, 0, ALL, degree)
        at += held.shape[0]

    rim_first[...] = active(rim[...], gains, 0).astype(jnp.bfloat16)
    near = slice(0, OUT - OWN)
    ended = slice(0, 2 * EAST)
    total[ended] = ((end_sum[...] + dot(end_links[...], rim_first[near])) * sixth).astype(jnp.bfloat16)
    total[2 * EAST :] = (
        (dot(ring[:, :OWN], first[...]) + dot(ring[:, OWN:], rim_first[...])) * sixth
    ).astype(jnp.bfloat16)
    part[ended] = end_part[...]
    part[2 * EAST :] = dot(rim_first[near], w_self[0])
    v = rest(total[...], part[...], w_nbr, w_out, 0)
    own = slice(0, OWN)
    column = slice(2, 2 + EAST)
    v_ends = v[ended] + jnp.concatenate([sides[0, column], sides[1, column]], axis=0)
    second[OWN:] = active(v[2 * EAST :] + rim[near], gains, 1).astype(jnp.bfloat16)
    a_ends = active(v_ends, gains, 1)

    for out, new in ((x1, v_ends), (a1, a_ends)):
        for tile in range(out.shape[0]):
            for side, place_in in enumerate((0, NORTH - 1)):
                out[tile, pl.ds(place_in, EAST, stride=NORTH)] = new[
                    side * EAST : (side + 1) * EAST, tile * LANES : (tile + 1) * LANES
                ]
    second[own] = joined(a1).astype(jnp.bfloat16)
    sums = (dot(links[...], second[...]) * sixth).astype(jnp.bfloat16)
    v = joined(x1) + rest(sums, dot(second[own], w_self[1]), w_nbr, w_out, 1)
    value = dot(norm(v).astype(jnp.bfloat16), w_dec[...]).astype(jnp.bfloat16)
    preds[...] = value
    sent[...] = value


def score_share(mine, truth, copies):
    members, share, _ = mine.shape
    denom = 2.0 * members * (members - 1)
    held = [mine[one].astype(jnp.float32) for one in range(members)]
    goal = truth[pl.ds(pl.multiple_of(here("member") * share, share), share)].astype(jnp.float32)
    skill = jnp.zeros(goal.shape, jnp.float32)
    spread = jnp.zeros(goal.shape, jnp.float32)
    for one in range(members):
        skill = skill + jnp.abs(held[one] - goal)
        for two in range(one):
            spread = spread + jnp.abs(held[one] - held[two])
    score = (skill * (1.0 / members) - spread * (2.0 / denom)).astype(jnp.bfloat16)
    for one in range(members):
        copies[one] = score


def swap(far, near, axis):
    peers = lax.axis_size(axis)
    pairs = [[(i, i + 1), (i + 1, i)] for i in range(peers - 1)]
    return (
        lax.ppermute(far, axis, sum(pairs[1::2], [])),
        lax.ppermute(near, axis, sum(pairs[0::2], [])),
    )


def local(states, noises, codes, target, w_self, w_nbr, w_out, w_scale, w_shift, w_dec):
    width = states.shape[-1]
    degree = codes.shape[-1]
    variables = w_dec.shape[-1]
    layers = w_self.shape[0]
    x = states.reshape(OWN, width)
    sizes = (lax.axis_size("sx") * EAST, lax.axis_size("sy") * NORTH)
    vmem = pl.BlockSpec(memory_space=pltpu.VMEM)

    def like(shape, dtype=jnp.bfloat16):
        return jax.ShapeDtypeStruct(shape, dtype)

    def limits(mib):
        return pltpu.CompilerParams(vmem_limit_bytes=mib << 20)

    def cost(flops, size):
        return pl.CostEstimate(flops=flops, bytes_accessed=size, transcendentals=0)

    slots = codes.transpose(2, 1, 0)
    far_row, near_row = swap(
        *pl.pallas_call(
            functools.partial(rows_out, degree),
            grid=(1,),
            out_shape=(like((3 * NORTH, width)),) * 2,
            in_specs=[
                pl.BlockSpec((2 * NORTH, width), lambda i: (0, 0)),
                pl.BlockSpec((2 * NORTH, width), lambda i: (OWN // (2 * NORTH) - 1, 0)),
                pl.BlockSpec(slots.shape, lambda i: (0, 0, 0)),
            ],
            out_specs=(pl.BlockSpec((3 * NORTH, width), lambda i: (0, 0)),) * 2,
            compiler_params=pltpu.CompilerParams(vmem_limit_bytes=55104 << 10),
            name="rows_out",
        )(x, x, slots),
        "sx",
    )

    index = neighbours(
        slots,
        lax.broadcasted_iota(jnp.int32, slots.shape, 2),
        lax.broadcasted_iota(jnp.int32, slots.shape, 1),
        (here("sx"), here("sy")),
        sizes,
    )
    coded = (index + 1 + CODE * slots).transpose(2, 1, 0).reshape(OWN, degree)
    sides = pl.pallas_call(
        functools.partial(collect, degree),
        out_shape=like((2, SIDE, width), jnp.float32),
        in_specs=[vmem] * 2,
        out_specs=vmem,
        scratch_shapes=[pltpu.VMEM((2, PAD, LANES), jnp.float32)],
        compiler_params=limits(8),
        cost_estimate=cost(1 << 20, 1 << 25),
        name="collect",
    )(x, coded)

    sent = pl.pallas_call(
        columns_out,
        out_shape=(like((SIDE, width)),) * 2,
        in_specs=[pl.BlockSpec(memory_space=pl.ANY)] + [vmem] * 3,
        out_specs=(vmem,) * 2,
        scratch_shapes=[pltpu.VMEM((2, SIDE, width), jnp.float32)],
        compiler_params=limits(8),
        cost_estimate=cost(1 << 20, 1 << 25),
        name="columns_out",
    )(w_out, sides, far_row, near_row)
    far_column, near_column = swap(*sent, "sy")

    halves = like((2 * EAST, width), jnp.float32)
    whole = like((width // LANES, OWN, LANES), jnp.float32)
    first, links, gains, end_links, end_sum, end_part, x1, a1 = pl.pallas_call(
        functools.partial(prepare, degree),
        out_shape=(
            like((OWN, width)),
            like((OWN, OUT)),
            like((2 * layers, width), jnp.float32),
            like((2 * EAST, OUT - OWN)),
            halves,
            halves,
            whole,
            whole,
        ),
        in_specs=[vmem] * 10 + [pl.BlockSpec(memory_space=pl.ANY)],
        out_specs=(vmem,) * 8,
        scratch_shapes=[
            pltpu.VMEM((OWN, width), jnp.float32),
            pltpu.VMEM((OWN, width), jnp.float32),
            pltpu.VMEM((OUT - OWN, width), jnp.bfloat16),
        ],
        compiler_params=limits(16),
        cost_estimate=cost(1 << 24, 1 << 25),
        name="prepare",
    )(x, coded, noises, w_scale, w_shift, w_self, w_nbr, w_out, far_row, near_row, sent[1])

    busy = 2 * EAST + OUT - OWN
    preds, shares, _, _ = pl.pallas_call(
        functools.partial(advance, sizes, degree),
        out_shape=(like((OWN, variables)),) * 2 + (whole,) * 2,
        in_specs=[vmem] * 17,
        out_specs=(vmem,) * 4,
        input_output_aliases={6: 2, 7: 3},
        scratch_shapes=[
            pltpu.VMEM((ALL - OWN, width), jnp.bfloat16),
            pltpu.VMEM((OUT, width), jnp.bfloat16),
            pltpu.VMEM((busy, width), jnp.bfloat16),
            pltpu.VMEM((busy, width), jnp.float32),
            pltpu.VMEM((ALL - OWN, width), jnp.float32),
            pltpu.VMEM((OUT - OWN, ALL), jnp.bfloat16),
        ],
        compiler_params=limits(16),
        cost_estimate=cost(1 << 31, 1 << 23),
        name="advance",
    )(
        first, links, gains, end_links, end_sum, end_part, x1, a1, sides,
        far_row, near_row, far_column, near_column, w_self, w_nbr, w_out, w_dec,
    )

    members = lax.axis_size("member")
    share = OWN // members
    mine = lax.all_to_all(shares.reshape(members, share, variables), "member", 0, 0)
    copies = pl.pallas_call(
        score_share,
        out_shape=like(mine.shape),
        in_specs=[vmem] * 2,
        out_specs=vmem,
        compiler_params=limits(8),
        name="score_share",
    )(mine, target.reshape(OWN, variables))
    scores = lax.all_to_all(copies, "member", 0, 0).astype(jnp.float32)
    return (preds.reshape(1, EAST, NORTH, variables), scores.reshape(target.shape))


def solution(mesh):
    placed = (
        P("member", "sx", "sy", None),
        P("member", None),
        P("sx", "sy", None),
        P("sx", "sy", None),
        P(),
        P(),
        P(),
        P(),
        P(),
        P(),
    )
    return jax.shard_map(
        local,
        mesh=mesh,
        in_specs=placed,
        out_specs=(P("member", "sx", "sy", None), P("sx", "sy", None)),
        check_vma=False,
    )
```

```python
import functools

import jax
import jax.numpy as jnp
from jax import lax
from jax.experimental import pallas as pl
from jax.experimental.pallas import tpu as pltpu
from jax.sharding import PartitionSpec as P

EAST = 32
NORTH = 16
OWN = EAST * NORTH
LONG = EAST + 4
PAD = 48
CODED = 40
FAR = 56
SIDE = 96
LANES = 128
CODE = 1024
OUT = OWN + 2 * NORTH + 2 * PAD
ALL = OUT + 2 * NORTH + 2 * PAD
EPS = 1e-05


def place(row, column):
    inner = jnp.where(
        (row >= 0) & (row < EAST),
        row * NORTH + column,
        jnp.where(
            row == -1,
            OWN + column,
            jnp.where(
                row == EAST,
                OWN + NORTH + column,
                jnp.where(row == -2, OUT + column, OUT + NORTH + column),
            ),
        ),
    )
    side = jnp.where(
        column == -1,
        OWN + 2 * NORTH,
        jnp.where(
            column == NORTH,
            OWN + 2 * NORTH + PAD,
            jnp.where(column == -2, OUT + 2 * NORTH, OUT + 2 * NORTH + PAD),
        ),
    )
    return jnp.where((column >= 0) & (column < NORTH), inner, side + row + 2)


def neighbours(codes, row, column, spot, sizes):
    third = (codes >= 3).astype(jnp.int32) + (codes >= 6).astype(jnp.int32)
    to_row = row + third - 1
    to_column = column + (codes - 3 * third) - 1
    east = spot[0] * EAST + to_row
    north = spot[1] * NORTH + to_column
    real = (east >= 0) & (east < sizes[0]) & (north >= 0) & (north < sizes[1])
    real = real & (row >= -1) & (row <= EAST)
    return jnp.where(real, place(to_row, to_column), -1)


def counted(slots, at, width):
    lanes = lax.broadcasted_iota(jnp.int32, (slots[0].shape[0], width), 1) + at
    total = jnp.zeros(lanes.shape, jnp.float32)
    for slot in slots:
        total = total + jnp.where(lanes == slot, 1.0, 0.0)
    return total.astype(jnp.bfloat16)


def apart(index, degree):
    return [index[:, slot : slot + 1] for slot in range(degree)]


def norm(x):
    away = x - jnp.mean(x, axis=-1, keepdims=True)
    var = jnp.mean(away * away, axis=-1, keepdims=True)
    return away * lax.rsqrt(var + EPS)


def dot(a, b):
    return jnp.dot(a, b, preferred_element_type=jnp.float32)


def here(axis):
    return lax.axis_index(axis).astype(jnp.int32)


def rows_out(degree, top, bottom, codes, far_out, near_out):
    lane = lax.broadcasted_iota(jnp.int32, (NORTH, LANES), 1)
    lines = []
    for row in (0, EAST - 1):
        named = jnp.zeros((NORTH, LANES), jnp.int32)
        for slot in range(degree):
            named = jnp.where(lane == slot, codes[slot, :, row : row + 1], named)
        lines.append(named.astype(jnp.float32).astype(jnp.bfloat16))
    odd = here("sx") % 2 == 1
    for out, is_top in ((far_out, jnp.logical_not(odd)), (near_out, odd)):
        out[: 2 * NORTH] = jnp.where(is_top, top[...], bottom[...])
        out[2 * NORTH :] = jnp.zeros((NORTH, out.shape[1]), jnp.bfloat16)
        out[2 * NORTH :, :LANES] = jnp.where(is_top, lines[0], lines[1])


def sorted_by(axis, far, near):
    odd = here(axis) % 2 == 1
    far, near = (far[...].astype(jnp.float32), near[...].astype(jnp.float32))
    return jnp.where(odd, near, far), jnp.where(odd, far, near)


def by_row(slots, column, turned):
    turned[...] = jnp.zeros(turned.shape, jnp.float32)
    for slot in range(slots.shape[0]):
        turned[slot : slot + 1, :EAST] = slots[slot, column : column + 1].astype(jnp.float32)
    return turned[...].T[:EAST]


def collect(degree, x, coded, sides, named):
    sides[...] = jnp.zeros(sides.shape, jnp.float32)
    named[...] = jnp.zeros(named.shape, jnp.float32)
    lines = 8
    rows = lines * NORTH
    for part in range(EAST // lines):
        span = slice(part * rows, (part + 1) * rows)
        grid = x[span].astype(jnp.float32).reshape(lines, NORTH, x.shape[1])
        held = coded[span].reshape(lines, NORTH, degree)
        at = 2 + part * lines
        for side, (near, far) in enumerate(((0, 1), (NORTH - 1, NORTH - 2))):
            sides[side, at : at + lines] = grid[:, near]
            sides[side, FAR + at : FAR + at + lines] = grid[:, far]
            named[side, at : at + lines, :degree] = (held[:, near] & (CODE - 1)).astype(jnp.float32)
    for side in range(2):
        for part in range(PAD // 16):
            sides[side, CODED:FAR, part * LANES : (part + 1) * LANES] = named[
                side, part * 16 : (part + 1) * 16
            ]


def active(v, gains, layer):
    return norm(v) * gains[2 * layer : 2 * layer + 1] + gains[2 * layer + 1 : 2 * layer + 2]


def rest(total, part, w_nbr, w_out, layer):
    hidden = jax.nn.silu(part + dot(total, w_nbr[layer])).astype(jnp.bfloat16)
    return dot(hidden, w_out[layer])


def ends(v):
    grid = v.reshape(EAST, NORTH, v.shape[-1])
    return jnp.concatenate([grid[:, 0], grid[:, NORTH - 1]], axis=0)


def split(out, v):
    for tile in range(out.shape[0]):
        out[tile] = v[:, tile * LANES : (tile + 1) * LANES]


def joined(tiles):
    return jnp.concatenate([tiles[tile] for tile in range(tiles.shape[0])], axis=1)


def own_neighbours(arrived, row0, column0, sizes, degree):
    if column0 == 0:
        held = arrived[2 * NORTH : 3 * NORTH, :LANES]
    else:
        held = jnp.concatenate(
            [arrived[CODED:FAR, i * LANES : (i + 1) * LANES] for i in range(PAD // 16)], axis=0
        )
    held = held[:, :degree].astype(jnp.int32)
    step = lax.broadcasted_iota(jnp.int32, held.shape, 0)
    if column0 == 0:
        row, column = (jnp.full(held.shape, row0, jnp.int32), step)
    else:
        row, column = (row0 + step, jnp.full(held.shape, column0, jnp.int32))
    index = neighbours(held, row, column, (here("sx"), here("sy")), sizes)
    return counted(apart(index, degree), 0, ALL)


def prepare(
    sizes, x, slots, noise, w_scale, w_shift, w_self, w_nbr, w_out, far_row, near_row, sent,
    first, gains, late_links, end_links, end_sum, end_part, x1, sum1, part1,
    rim_rows, ring_rows, rim_x, links, own_sum, own_part, rim, index, turned,
):
    degree = slots.shape[0]
    for layer in range(w_scale.shape[0]):
        for at, w in enumerate((w_scale, w_shift)):
            gains[2 * layer + at : 2 * layer + at + 1] = (1.0 - at) + jnp.dot(
                noise[...], w[layer], precision=lax.Precision.HIGHEST,
                preferred_element_type=jnp.float32,
            )
    links[...] = jnp.zeros(links.shape, jnp.bfloat16)
    first[...] = active(x[...].astype(jnp.float32), gains, 0).astype(jnp.bfloat16)
    own_part[...] = dot(first[...], w_self[0])

    found = neighbours(
        slots[...],
        lax.broadcasted_iota(jnp.int32, slots.shape, 2),
        lax.broadcasted_iota(jnp.int32, slots.shape, 1),
        (here("sx"), here("sy")),
        sizes,
    )
    index[0] = found
    line, step = (found // NORTH, found % NORTH)
    end = jnp.where(step == 0, line, jnp.where(step == NORTH - 1, EAST + line, -1))
    index[1] = jnp.where((found >= 0) & (found < OWN), end, -1)
    for row in range(EAST):
        span = slice(row * NORTH, (row + 1) * NORTH)
        named, ended = (
            [index[which, slot, :, row : row + 1] for slot in range(degree)] for which in (0, 1)
        )
        tiles = {max(row - 1, 0) * NORTH // LANES, min(row + 1, EAST - 1) * NORTH // LANES}
        for tile in sorted(tiles) + [OWN // LANES]:
            links[span, tile * LANES : (tile + 1) * LANES] = counted(named, tile * LANES, LANES)
        late_links[span, LANES:] = counted(ended, 0, LANES)
    late_links[:, :LANES] = links[:, OWN:]
    for side, column in enumerate((0, NORTH - 1)):
        ends_found = by_row(index.at[0], column, turned.at[side]).astype(jnp.int32)
        end_links[side * EAST : (side + 1) * EAST] = counted(
            apart(ends_found, degree), OWN, OUT - OWN
        )

    own_sum[...] = dot(links[:, :OWN], first[...])
    end_part[...] = ends(own_part[...])
    end_sum[...] = ends(own_sum[...])
    top, bottom = sorted_by("sx", far_row, near_row)
    nearer = jnp.concatenate([top[NORTH : 2 * NORTH], bottom[:NORTH]], axis=0)
    rim_x[...] = nearer
    rim_rows[: 2 * NORTH] = active(nearer, gains, 0).astype(jnp.bfloat16)
    rim_rows[2 * NORTH :] = active(
        jnp.concatenate([top[:NORTH], bottom[NORTH : 2 * NORTH]], axis=0), gains, 0
    ).astype(jnp.bfloat16)
    rim[: 2 * NORTH] = rim_rows[: 2 * NORTH]
    rim[2 * NORTH :] = jnp.zeros((rim.shape[0] - 2 * NORTH, rim.shape[1]), jnp.bfloat16)
    total = own_sum[...] + dot(links[:, OWN:], rim[...])
    total = (total * (1.0 / degree)).astype(jnp.bfloat16)
    v = x[...].astype(jnp.float32) + rest(total, own_part[...], w_nbr, w_out, 0)
    split(x1, v)
    step = lax.broadcasted_iota(jnp.int32, (OWN, 1), 0) % NORTH
    inner = (step > 0) & (step < NORTH - 1)
    a1 = jnp.where(inner, active(v, gains, 1), 0.0).astype(jnp.bfloat16)
    sum1[...] = dot(links[:, :OWN], a1)
    split(part1, dot(a1, w_self[1]))
    ring_rows[:NORTH] = own_neighbours(top, -1, 0, sizes, degree)
    ring_rows[NORTH:] = own_neighbours(bottom, EAST, 0, sizes, degree)


def columns_out(w_out, sides, far_row, near_row, far_out, near_out, lines):
    top, bottom = sorted_by("sx", far_row, near_row)
    for side, (near, far) in enumerate(((0, 1), (NORTH - 1, NORTH - 2))):
        lines[side] = sides[side]
        for at, column in ((0, near), (FAR, far)):
            for step, source, row in (
                (0, top, 0), (1, top, 1), (EAST + 2, bottom, 0), (EAST + 3, bottom, 1)
            ):
                picked = row * NORTH + column
                lines[side, at + step : at + step + 1] = source[picked : picked + 1]
        picked = 2 * NORTH + near
        lines[side, CODED + 1 : CODED + 2, :LANES] = top[picked : picked + 1, :LANES]
        part, line = divmod(EAST + 2, 16)
        lines[side, CODED + line : CODED + line + 1, part * LANES : (part + 1) * LANES] = bottom[
            picked : picked + 1, :LANES
        ]
    odd = here("sy") % 2
    far_out[...] = lines[odd].astype(jnp.bfloat16)
    near_out[...] = lines[1 - odd].astype(jnp.bfloat16)


def advance(
    sizes, degree, first, gains, late_links, end_links, end_sum, end_part, old_x1, sum1, old_part1,
    rim_rows, ring_rows, rim_x, sides, far_column, near_column, w_self, w_nbr, w_out, w_dec,
    preds, sent, x1, part1, rim_first, late, total, part, ring,
):
    sixth = 1.0 / degree
    west, east = sorted_by("sy", far_column, near_column)
    nearer = jnp.concatenate([west[:PAD], east[:PAD]], axis=0)
    gap = jnp.zeros((PAD - SIDE + FAR, west.shape[1]), jnp.float32)
    farther = jnp.concatenate([west[FAR:], gap, east[FAR:], gap], axis=0)
    near = slice(0, OUT - OWN)
    rows = 2 * NORTH
    rim_first[:rows] = rim_rows[:rows]
    rim_first[rows : OUT - OWN] = active(nearer, gains, 0).astype(jnp.bfloat16)
    rim_first[OUT - OWN : OUT - OWN + rows] = rim_rows[rows:]
    rim_first[OUT - OWN + rows :] = active(farther, gains, 0).astype(jnp.bfloat16)
    ring[:rows] = ring_rows[...]
    ring[rows : rows + PAD] = own_neighbours(west, -2, -1, sizes, degree)
    ring[rows + PAD :] = own_neighbours(east, -2, NORTH, sizes, degree)

    ended = slice(0, 2 * EAST)
    total[ended] = ((end_sum[...] + dot(end_links[...], rim_first[near])) * sixth).astype(jnp.bfloat16)
    total[2 * EAST :] = (
        (dot(ring[:, :OWN], first[...]) + dot(ring[:, OWN:], rim_first[...])) * sixth
    ).astype(jnp.bfloat16)
    part[ended] = end_part[...]
    part[2 * EAST :] = dot(rim_first[near], w_self[0])
    v = rest(total[...], part[...], w_nbr, w_out, 0)
    column = slice(2, 2 + EAST)
    v_ends = v[ended] + jnp.concatenate([sides[0, column], sides[1, column]], axis=0)
    v_ring = v[2 * EAST :] + jnp.concatenate([rim_x[...], nearer], axis=0)
    a_ends = active(v_ends, gains, 1).astype(jnp.bfloat16)
    late[near] = active(v_ring, gains, 1).astype(jnp.bfloat16)
    late[OUT - OWN : OUT - OWN + 2 * EAST] = a_ends
    late[OUT - OWN + 2 * EAST :] = jnp.zeros((LANES - 2 * EAST, late.shape[1]), jnp.bfloat16)

    for out, new in ((x1, v_ends), (part1, dot(a_ends, w_self[1]))):
        for tile in range(out.shape[0]):
            for side, place_in in enumerate((0, NORTH - 1)):
                out[tile, pl.ds(place_in, EAST, stride=NORTH)] = new[
                    side * EAST : (side + 1) * EAST, tile * LANES : (tile + 1) * LANES
                ]
    sums = ((sum1[...] + dot(late_links[...], late[...])) * sixth).astype(jnp.bfloat16)
    v = joined(x1) + rest(sums, joined(part1), w_nbr, w_out, 1)
    value = dot(norm(v).astype(jnp.bfloat16), w_dec[...]).astype(jnp.bfloat16)
    preds[...] = value
    sent[...] = value


def score_share(mine, truth, copies):
    members, share, _ = mine.shape
    denom = 2.0 * members * (members - 1)
    held = [mine[one].astype(jnp.float32) for one in range(members)]
    goal = truth[pl.ds(pl.multiple_of(here("member") * share, share), share)].astype(jnp.float32)
    skill = jnp.zeros(goal.shape, jnp.float32)
    spread = jnp.zeros(goal.shape, jnp.float32)
    for one in range(members):
        skill = skill + jnp.abs(held[one] - goal)
        for two in range(one):
            spread = spread + jnp.abs(held[one] - held[two])
    score = (skill * (1.0 / members) - spread * (2.0 / denom)).astype(jnp.bfloat16)
    for one in range(members):
        copies[one] = score


def swap(far, near, axis):
    peers = lax.axis_size(axis)
    pairs = [[(i, i + 1), (i + 1, i)] for i in range(peers - 1)]
    return (
        lax.ppermute(far, axis, sum(pairs[1::2], [])),
        lax.ppermute(near, axis, sum(pairs[0::2], [])),
    )


def local(states, noises, codes, target, w_self, w_nbr, w_out, w_scale, w_shift, w_dec):
    width = states.shape[-1]
    degree = codes.shape[-1]
    variables = w_dec.shape[-1]
    layers = w_self.shape[0]
    x = states.reshape(OWN, width)
    sizes = (lax.axis_size("sx") * EAST, lax.axis_size("sy") * NORTH)
    vmem = pl.BlockSpec(memory_space=pltpu.VMEM)

    def like(shape, dtype=jnp.bfloat16):
        return jax.ShapeDtypeStruct(shape, dtype)

    def limits(mib):
        return pltpu.CompilerParams(vmem_limit_bytes=mib << 20)

    def cost(flops, size):
        return pl.CostEstimate(flops=flops, bytes_accessed=size, transcendentals=0)

    slots = codes.transpose(2, 1, 0)
    far_row, near_row = swap(
        *pl.pallas_call(
            functools.partial(rows_out, degree),
            grid=(1,),
            out_shape=(like((3 * NORTH, width)),) * 2,
            in_specs=[
                pl.BlockSpec((2 * NORTH, width), lambda i: (0, 0)),
                pl.BlockSpec((2 * NORTH, width), lambda i: (OWN // (2 * NORTH) - 1, 0)),
                pl.BlockSpec(slots.shape, lambda i: (0, 0, 0)),
            ],
            out_specs=(pl.BlockSpec((3 * NORTH, width), lambda i: (0, 0)),) * 2,
            compiler_params=pltpu.CompilerParams(vmem_limit_bytes=55104 << 10),
            name="rows_out",
        )(x, x, slots),
        "sx",
    )

    coded = (slots + CODE * here("sx")).transpose(2, 1, 0).reshape(OWN, degree)
    sides = pl.pallas_call(
        functools.partial(collect, degree),
        out_shape=like((2, SIDE, width), jnp.float32),
        in_specs=[vmem] * 2,
        out_specs=vmem,
        scratch_shapes=[pltpu.VMEM((2, PAD, LANES), jnp.float32)],
        compiler_params=limits(8),
        cost_estimate=cost(1 << 20, 1 << 25),
        name="collect",
    )(x, coded)

    sent = pl.pallas_call(
        columns_out,
        out_shape=(like((SIDE, width)),) * 2,
        in_specs=[pl.BlockSpec(memory_space=pl.ANY)] + [vmem] * 3,
        out_specs=(vmem,) * 2,
        scratch_shapes=[pltpu.VMEM((2, SIDE, width), jnp.float32)],
        compiler_params=limits(8),
        cost_estimate=cost(1 << 20, 1 << 25),
        name="columns_out",
    )(w_out, sides, far_row, near_row)
    far_column, near_column = swap(*sent, "sy")

    halves = like((2 * EAST, width), jnp.float32)
    whole = like((width // LANES, OWN, LANES), jnp.float32)
    square = pltpu.VMEM((OWN, width), jnp.float32)
    (
        first, gains, late_links, end_links, end_sum, end_part, x1, sum1, part1,
        rim_rows, ring_rows, rim_x,
    ) = pl.pallas_call(
        functools.partial(prepare, sizes),
        out_shape=(
            like((OWN, width)),
            like((2 * layers, width), jnp.float32),
            like((OWN, 2 * LANES)),
            like((2 * EAST, OUT - OWN)),
            halves,
            halves,
            whole,
            like((OWN, width), jnp.float32),
            whole,
            like((4 * NORTH, width)),
            like((2 * NORTH, ALL)),
            like((2 * NORTH, width), jnp.float32),
        ),
        in_specs=[vmem] * 10 + [pl.BlockSpec(memory_space=pl.ANY)],
        out_specs=(vmem,) * 12,
        scratch_shapes=[
            pltpu.VMEM((OWN, OUT), jnp.bfloat16),
            square,
            square,
            pltpu.VMEM((OUT - OWN, width), jnp.bfloat16),
            pltpu.VMEM((2,) + slots.shape, jnp.int32),
            pltpu.VMEM((2, 8, LANES), jnp.float32),
        ],
        compiler_params=limits(16),
        cost_estimate=cost(1 << 24, 1 << 25),
        name="prepare",
    )(x, slots, noises, w_scale, w_shift, w_self, w_nbr, w_out, far_row, near_row, sent[1])

    busy = 2 * EAST + OUT - OWN
    preds, shares, _, _ = pl.pallas_call(
        functools.partial(advance, sizes, degree),
        out_shape=(like((OWN, variables)),) * 2 + (whole,) * 2,
        in_specs=[vmem] * 19,
        out_specs=(vmem,) * 4,
        input_output_aliases={6: 2, 8: 3},
        scratch_shapes=[
            pltpu.VMEM((ALL - OWN, width), jnp.bfloat16),
            pltpu.VMEM((2 * LANES, width), jnp.bfloat16),
            pltpu.VMEM((busy, width), jnp.bfloat16),
            pltpu.VMEM((busy, width), jnp.float32),
            pltpu.VMEM((OUT - OWN, ALL), jnp.bfloat16),
        ],
        compiler_params=limits(16),
        cost_estimate=cost(1 << 31, 1 << 23),
        name="advance",
    )(
        first, gains, late_links, end_links, end_sum, end_part, x1, sum1, part1,
        rim_rows, ring_rows, rim_x, sides, far_column, near_column, w_self, w_nbr, w_out, w_dec,
    )

    members = lax.axis_size("member")
    share = OWN // members
    mine = lax.all_to_all(shares.reshape(members, share, variables), "member", 0, 0)
    copies = pl.pallas_call(
        score_share,
        out_shape=like(mine.shape),
        in_specs=[vmem] * 2,
        out_specs=vmem,
        compiler_params=limits(8),
        name="score_share",
    )(mine, target.reshape(OWN, variables))
    scores = lax.all_to_all(copies, "member", 0, 0).astype(jnp.float32)
    return (preds.reshape(1, EAST, NORTH, variables), scores.reshape(target.shape))


def solution(mesh):
    placed = (
        P("member", "sx", "sy", None),
        P("member", None),
        P("sx", "sy", None),
        P("sx", "sy", None),
        P(),
        P(),
        P(),
        P(),
        P(),
        P(),
    )
    return jax.shard_map(
        local,
        mesh=mesh,
        in_specs=placed,
        out_specs=(P("member", "sx", "sy", None), P("sx", "sy", None)),
        check_vma=False,
    )
```

```python
import functools

import jax
import jax.numpy as jnp
from jax import lax
from jax.experimental import pallas as pl
from jax.experimental.pallas import tpu as pltpu
from jax.sharding import PartitionSpec as P

EAST = 32
NORTH = 16
OWN = EAST * NORTH
LONG = EAST + 4
PAD = 48
CODED = 40
FAR = 56
SIDE = 96
LANES = 128
CODE = 1024
OUT = OWN + 2 * NORTH + 2 * PAD
ALL = OUT + 2 * NORTH + 2 * PAD
EPS = 1e-05


def place(row, column):
    inner = jnp.where(
        (row >= 0) & (row < EAST),
        row * NORTH + column,
        jnp.where(
            row == -1,
            OWN + column,
            jnp.where(
                row == EAST,
                OWN + NORTH + column,
                jnp.where(row == -2, OUT + column, OUT + NORTH + column),
            ),
        ),
    )
    side = jnp.where(
        column == -1,
        OWN + 2 * NORTH,
        jnp.where(
            column == NORTH,
            OWN + 2 * NORTH + PAD,
            jnp.where(column == -2, OUT + 2 * NORTH, OUT + 2 * NORTH + PAD),
        ),
    )
    return jnp.where((column >= 0) & (column < NORTH), inner, side + row + 2)


def neighbours(codes, row, column, spot, sizes):
    third = (codes >= 3).astype(jnp.int32) + (codes >= 6).astype(jnp.int32)
    to_row = row + third - 1
    to_column = column + (codes - 3 * third) - 1
    east = spot[0] * EAST + to_row
    north = spot[1] * NORTH + to_column
    real = (east >= 0) & (east < sizes[0]) & (north >= 0) & (north < sizes[1])
    real = real & (row >= -1) & (row <= EAST)
    return jnp.where(real, place(to_row, to_column), -1)


def counted(slots, at, width):
    lanes = lax.broadcasted_iota(jnp.int32, (slots[0].shape[0], width), 1) + at
    total = jnp.zeros(lanes.shape, jnp.float32)
    for slot in slots:
        total = total + jnp.where(lanes == slot, 1.0, 0.0)
    return total.astype(jnp.bfloat16)


def apart(index, degree):
    return [index[:, slot : slot + 1] for slot in range(degree)]


def norm(x):
    away = x - jnp.mean(x, axis=-1, keepdims=True)
    var = jnp.mean(away * away, axis=-1, keepdims=True)
    return away * lax.rsqrt(var + EPS)


def dot(a, b):
    return jnp.dot(a, b, preferred_element_type=jnp.float32)


def here(axis):
    return lax.axis_index(axis).astype(jnp.int32)


def rows_out(degree, top, bottom, codes, far_out, near_out):
    lane = lax.broadcasted_iota(jnp.int32, (NORTH, LANES), 1)
    lines = []
    for row in (0, EAST - 1):
        named = jnp.zeros((NORTH, LANES), jnp.int32)
        for slot in range(degree):
            named = jnp.where(lane == slot, codes[slot, :, row : row + 1], named)
        lines.append(named.astype(jnp.float32).astype(jnp.bfloat16))
    odd = here("sx") % 2 == 1
    for out, is_top in ((far_out, jnp.logical_not(odd)), (near_out, odd)):
        out[: 2 * NORTH] = jnp.where(is_top, top[...], bottom[...])
        out[2 * NORTH :] = jnp.zeros((NORTH, out.shape[1]), jnp.bfloat16)
        out[2 * NORTH :, :LANES] = jnp.where(is_top, lines[0], lines[1])


def hand_on(message, *others):
    out = others[-1]
    out[...] = message[...]


def sorted_by(axis, far, near):
    odd = here(axis) % 2 == 1
    far, near = (far[...].astype(jnp.float32), near[...].astype(jnp.float32))
    return jnp.where(odd, near, far), jnp.where(odd, far, near)


def by_row(slots, column, turned):
    turned[...] = jnp.zeros(turned.shape, jnp.float32)
    for slot in range(slots.shape[0]):
        turned[slot : slot + 1, :EAST] = slots[slot, column : column + 1].astype(jnp.float32)
    return turned[...].T[:EAST]


def collect(degree, x, coded, sides, named):
    sides[...] = jnp.zeros(sides.shape, jnp.float32)
    named[...] = jnp.zeros(named.shape, jnp.float32)
    lines = 8
    rows = lines * NORTH
    for part in range(EAST // lines):
        span = slice(part * rows, (part + 1) * rows)
        grid = x[span].astype(jnp.float32).reshape(lines, NORTH, x.shape[1])
        held = coded[span].reshape(lines, NORTH, degree)
        at = 2 + part * lines
        for side, (near, far) in enumerate(((0, 1), (NORTH - 1, NORTH - 2))):
            sides[side, at : at + lines] = grid[:, near]
            sides[side, FAR + at : FAR + at + lines] = grid[:, far]
            named[side, at : at + lines, :degree] = (held[:, near] & (CODE - 1)).astype(jnp.float32)
    for side in range(2):
        for part in range(PAD // 16):
            sides[side, CODED:FAR, part * LANES : (part + 1) * LANES] = named[
                side, part * 16 : (part + 1) * 16
            ]


def active(v, gains, layer):
    return norm(v) * gains[2 * layer : 2 * layer + 1] + gains[2 * layer + 1 : 2 * layer + 2]


def rest(total, part, w_nbr, w_out, layer):
    hidden = jax.nn.silu(part + dot(total, w_nbr[layer])).astype(jnp.bfloat16)
    return dot(hidden, w_out[layer])


def ends(v):
    grid = v.reshape(EAST, NORTH, v.shape[-1])
    return jnp.concatenate([grid[:, 0], grid[:, NORTH - 1]], axis=0)


FOUR = (0, NORTH - 1, 1, NORTH - 2)


def begin(
    sizes, x, slots, noise, w_scale, w_shift, first, gains, links, four_links, own_sum,
    index, turned,
):
    degree = slots.shape[0]
    for layer in range(w_scale.shape[0]):
        for at, w in enumerate((w_scale, w_shift)):
            gains[2 * layer + at : 2 * layer + at + 1] = (1.0 - at) + jnp.dot(
                noise[...], w[layer], precision=lax.Precision.HIGHEST,
                preferred_element_type=jnp.float32,
            )
    links[...] = jnp.zeros(links.shape, jnp.bfloat16)
    first[...] = active(x[...].astype(jnp.float32), gains, 0).astype(jnp.bfloat16)
    found = neighbours(
        slots[...],
        lax.broadcasted_iota(jnp.int32, slots.shape, 2),
        lax.broadcasted_iota(jnp.int32, slots.shape, 1),
        (here("sx"), here("sy")),
        sizes,
    )
    index[0] = found
    line, step = (found // NORTH, found % NORTH)
    end = jnp.where(step == 0, line, jnp.where(step == NORTH - 1, EAST + line, -1))
    index[1] = jnp.where((found >= 0) & (found < OWN), end, -1)
    for row in range(EAST):
        span = slice(row * NORTH, (row + 1) * NORTH)
        named = [index[0, slot, :, row : row + 1] for slot in range(degree)]
        tiles = {max(row - 1, 0) * NORTH // LANES, min(row + 1, EAST - 1) * NORTH // LANES}
        for tile in sorted(tiles) + [OWN // LANES]:
            links[span, tile * LANES : (tile + 1) * LANES] = counted(named, tile * LANES, LANES)
    for part, column in enumerate(FOUR):
        for which, at in enumerate((OWN, 0)):
            turn = by_row(index.at[which], column, turned.at[2 * part + which])
            four_links[part * EAST : (part + 1) * EAST, which * LANES : (which + 1) * LANES] = (
                counted(apart(turn.astype(jnp.int32), degree), at, LANES)
            )
    own_sum[...] = dot(links[:, :OWN], first[...])


def own_neighbours(arrived, row0, column0, sizes, degree):
    if column0 == 0:
        held = arrived[2 * NORTH : 3 * NORTH, :LANES]
    else:
        held = jnp.concatenate(
            [arrived[CODED:FAR, i * LANES : (i + 1) * LANES] for i in range(PAD // 16)], axis=0
        )
    held = held[:, :degree].astype(jnp.int32)
    step = lax.broadcasted_iota(jnp.int32, held.shape, 0)
    if column0 == 0:
        row, column = (jnp.full(held.shape, row0, jnp.int32), step)
    else:
        row, column = (row0 + step, jnp.full(held.shape, column0, jnp.int32))
    index = neighbours(held, row, column, (here("sx"), here("sy")), sizes)
    return counted(apart(index, degree), 0, ALL)


def columns(v, which):
    grid = v.reshape(EAST, NORTH, v.shape[-1])
    return jnp.concatenate([grid[:, column] for column in which], axis=0)


def prepare(
    sizes, degree, x, first, gains, links, own_sum, w_self, w_nbr, w_out, w_dec,
    far_row, near_row, sent,
    end_sum, end_part, four_sum, two_part, two_x, mid, rim_rows, ring_rows, rim_x,
    total, part, rim, state,
):
    sixth = 1.0 / degree
    own = slice(0, OWN)
    top, bottom = sorted_by("sx", far_row, near_row)
    nearer = jnp.concatenate([top[NORTH : 2 * NORTH], bottom[:NORTH]], axis=0)
    rows = 2 * NORTH
    rim_x[...] = nearer
    rim_rows[:rows] = active(nearer, gains, 0).astype(jnp.bfloat16)
    rim_rows[rows:] = active(
        jnp.concatenate([top[:NORTH], bottom[NORTH : 2 * NORTH]], axis=0), gains, 0
    ).astype(jnp.bfloat16)
    rim[...] = jnp.zeros(rim.shape, jnp.bfloat16)
    rim[:rows] = rim_rows[:rows]
    rim[OUT - OWN : OUT - OWN + rows] = rim_rows[rows:]
    ring_rows[:NORTH] = own_neighbours(top, -1, 0, sizes, degree)
    ring_rows[NORTH:] = own_neighbours(bottom, EAST, 0, sizes, degree)

    part[own] = dot(first[...], w_self[0])
    end_part[...] = ends(part[own])
    end_sum[...] = ends(own_sum[...])
    part[OWN:] = dot(rim_rows[:rows], w_self[0])
    total[own] = (
        (own_sum[...] + dot(links[:, OWN:], rim[: OUT - OWN])) * sixth
    ).astype(jnp.bfloat16)
    total[OWN:] = (
        (dot(ring_rows[:, :OWN], first[...]) + dot(ring_rows[:, OWN:], rim[...])) * sixth
    ).astype(jnp.bfloat16)
    v = rest(total[...], part[...], w_nbr, w_out, 0)
    state[...] = x[...].astype(jnp.float32) + v[own]
    two_x[...] = columns(state[...], FOUR[2:])
    rim[:rows] = active(nearer + v[OWN:], gains, 1).astype(jnp.bfloat16)
    step = lax.broadcasted_iota(jnp.int32, (OWN, 1), 0) % NORTH
    inner = (step > 0) & (step < NORTH - 1)
    a1 = jnp.where(inner, active(state[...], gains, 1), 0.0).astype(jnp.bfloat16)
    sums = dot(links[:, :OWN], a1)
    four_sum[...] = columns(sums, FOUR)
    part[own] = dot(a1, w_self[1])
    two_part[...] = columns(part[own], FOUR[2:])
    sums = ((sums + dot(links[:, OWN:], rim[: OUT - OWN])) * sixth).astype(jnp.bfloat16)
    v = state[...] + rest(sums, part[own], w_nbr, w_out, 1)
    mid[...] = dot(norm(v).astype(jnp.bfloat16), w_dec[...])


def columns_out(w_out, gains, sides, far_row, near_row, far_out, near_out, lines):
    top, bottom = sorted_by("sx", far_row, near_row)
    for side, (near, far) in enumerate(((0, 1), (NORTH - 1, NORTH - 2))):
        lines[side] = sides[side]
        for at, column in ((0, near), (FAR, far)):
            for step, source, row in (
                (0, top, 0), (1, top, 1), (EAST + 2, bottom, 0), (EAST + 3, bottom, 1)
            ):
                picked = row * NORTH + column
                lines[side, at + step : at + step + 1] = source[picked : picked + 1]
        picked = 2 * NORTH + near
        lines[side, CODED + 1 : CODED + 2, :LANES] = top[picked : picked + 1, :LANES]
        part, line = divmod(EAST + 2, 16)
        lines[side, CODED + line : CODED + line + 1, part * LANES : (part + 1) * LANES] = bottom[
            picked : picked + 1, :LANES
        ]
    odd = here("sy") % 2
    far_out[...] = lines[odd].astype(jnp.bfloat16)
    near_out[...] = lines[1 - odd].astype(jnp.bfloat16)


def advance(
    sizes, degree, first, gains, four_links, end_sum, end_part, four_sum, two_part, two_x, old_mid,
    rim_rows, ring_rows, rim_x, sides, far_column, near_column, w_self, w_nbr, w_out, w_dec,
    preds, sent, mid, rim_first, late, total, part, ring,
):
    sixth = 1.0 / degree
    west, east = sorted_by("sy", far_column, near_column)
    nearer = jnp.concatenate([west[:PAD], east[:PAD]], axis=0)
    gap = jnp.zeros((PAD - SIDE + FAR, west.shape[1]), jnp.float32)
    farther = jnp.concatenate([west[FAR:], gap, east[FAR:], gap], axis=0)
    near = slice(0, OUT - OWN)
    rows = 2 * NORTH
    rim_first[:rows] = rim_rows[:rows]
    rim_first[rows : OUT - OWN] = active(nearer, gains, 0).astype(jnp.bfloat16)
    rim_first[OUT - OWN : OUT - OWN + rows] = rim_rows[rows:]
    rim_first[OUT - OWN + rows :] = active(farther, gains, 0).astype(jnp.bfloat16)
    ring[:rows] = ring_rows[...]
    ring[rows : rows + PAD] = own_neighbours(west, -2, -1, sizes, degree)
    ring[rows + PAD :] = own_neighbours(east, -2, NORTH, sizes, degree)

    ended = slice(0, 2 * EAST)
    total[ended] = ((end_sum[...] + dot(four_links[ended, :LANES], rim_first[near])) * sixth).astype(jnp.bfloat16)
    total[2 * EAST :] = (
        (dot(ring[:, :OWN], first[...]) + dot(ring[:, OWN:], rim_first[...])) * sixth
    ).astype(jnp.bfloat16)
    part[ended] = end_part[...]
    part[2 * EAST :] = dot(rim_first[near], w_self[0])
    v = rest(total[...], part[...], w_nbr, w_out, 0)
    column = slice(2, 2 + EAST)
    v_ends = v[ended] + jnp.concatenate([sides[0, column], sides[1, column]], axis=0)
    v_ring = v[2 * EAST :] + jnp.concatenate([rim_x[...], nearer], axis=0)
    a_ends = active(v_ends, gains, 1).astype(jnp.bfloat16)
    late[near] = active(v_ring, gains, 1).astype(jnp.bfloat16)
    late[OUT - OWN : OUT - OWN + 2 * EAST] = a_ends
    late[OUT - OWN + 2 * EAST :] = jnp.zeros((LANES - 2 * EAST, late.shape[1]), jnp.bfloat16)

    sums = ((four_sum[...] + dot(four_links[...], late[...])) * sixth).astype(jnp.bfloat16)
    own_part = jnp.concatenate([dot(a_ends, w_self[1]), two_part[...]], axis=0)
    v = jnp.concatenate([v_ends, two_x[...]], axis=0) + rest(sums, own_part, w_nbr, w_out, 1)
    value = dot(norm(v).astype(jnp.bfloat16), w_dec[...])
    for at, place_in in enumerate(FOUR):
        mid[pl.ds(place_in, EAST, stride=NORTH)] = value[at * EAST : (at + 1) * EAST]
    value = mid[...].astype(jnp.bfloat16)
    preds[...] = value
    sent[...] = value


def score_share(mine, truth, copies):
    members, share, _ = mine.shape
    denom = 2.0 * members * (members - 1)
    held = [mine[one].astype(jnp.float32) for one in range(members)]
    goal = truth[pl.ds(pl.multiple_of(here("member") * share, share), share)].astype(jnp.float32)
    skill = jnp.zeros(goal.shape, jnp.float32)
    spread = jnp.zeros(goal.shape, jnp.float32)
    for one in range(members):
        skill = skill + jnp.abs(held[one] - goal)
        for two in range(one):
            spread = spread + jnp.abs(held[one] - held[two])
    score = (skill * (1.0 / members) - spread * (2.0 / denom)).astype(jnp.bfloat16)
    for one in range(members):
        copies[one] = score


def swap(far, near, axis):
    peers = lax.axis_size(axis)
    pairs = [[(i, i + 1), (i + 1, i)] for i in range(peers - 1)]
    from_near = lax.ppermute(near, axis, sum(pairs[0::2], []))
    return lax.ppermute(far, axis, sum(pairs[1::2], [])), from_near


def local(states, noises, codes, target, w_self, w_nbr, w_out, w_scale, w_shift, w_dec):
    width = states.shape[-1]
    degree = codes.shape[-1]
    variables = w_dec.shape[-1]
    layers = w_self.shape[0]
    x = states.reshape(OWN, width)
    sizes = (lax.axis_size("sx") * EAST, lax.axis_size("sy") * NORTH)
    vmem = pl.BlockSpec(memory_space=pltpu.VMEM)

    def like(shape, dtype=jnp.bfloat16):
        return jax.ShapeDtypeStruct(shape, dtype)

    def limits(mib):
        return pltpu.CompilerParams(vmem_limit_bytes=mib << 20)

    def cost(flops, size):
        return pl.CostEstimate(flops=flops, bytes_accessed=size, transcendentals=0)

    slots = codes.transpose(2, 1, 0)
    far_out, near_out = (
        pl.pallas_call(
            functools.partial(rows_out, degree),
            grid=(1,),
            out_shape=(like((3 * NORTH, width)),) * 2,
            in_specs=[
                pl.BlockSpec((2 * NORTH, width), lambda i: (0, 0)),
                pl.BlockSpec((2 * NORTH, width), lambda i: (OWN // (2 * NORTH) - 1, 0)),
                pl.BlockSpec(slots.shape, lambda i: (0, 0, 0)),
            ],
            out_specs=(pl.BlockSpec((3 * NORTH, width), lambda i: (0, 0)),) * 2,
            compiler_params=pltpu.CompilerParams(vmem_limit_bytes=55104 << 10),
            name="rows_out",
        )(x, x, slots)
    )
    far_out = pl.pallas_call(
        hand_on,
        out_shape=like(far_out.shape),
        in_specs=[vmem] + [pl.BlockSpec(memory_space=pl.ANY)] * 4,
        out_specs=vmem,
        compiler_params=limits(8),
        name="hand_on",
    )(far_out, near_out, noises, w_scale, w_shift)
    far_row, near_row = swap(far_out, near_out, "sx")

    coded = (slots + CODE * here("sx")).transpose(2, 1, 0).reshape(OWN, degree)
    sides = pl.pallas_call(
        functools.partial(collect, degree),
        out_shape=like((2, SIDE, width), jnp.float32),
        in_specs=[vmem] * 2,
        out_specs=vmem,
        scratch_shapes=[pltpu.VMEM((2, PAD, LANES), jnp.float32)],
        compiler_params=limits(8),
        cost_estimate=cost(1 << 20, 1 << 25),
        name="collect",
    )(x, coded)

    wide = like((OWN, width), jnp.float32)
    halves = like((2 * EAST, width), jnp.float32)
    first, gains, links, four_links, own_sum = pl.pallas_call(
        functools.partial(begin, sizes),
        out_shape=(
            like((OWN, width)),
            like((2 * layers, width), jnp.float32),
            like((OWN, OUT)),
            like((4 * EAST, 2 * LANES)),
            wide,
        ),
        in_specs=[vmem] * 5,
        out_specs=(vmem,) * 5,
        scratch_shapes=[
            pltpu.VMEM((2,) + slots.shape, jnp.int32),
            pltpu.VMEM((8, 8, LANES), jnp.float32),
        ],
        compiler_params=limits(8),
        cost_estimate=cost(1 << 24, 1 << 24),
        name="begin",
    )(x, slots, noises, w_scale, w_shift)

    sent = pl.pallas_call(
        columns_out,
        out_shape=(like((SIDE, width)),) * 2,
        in_specs=[pl.BlockSpec(memory_space=pl.ANY)] * 2 + [vmem] * 3,
        out_specs=(vmem,) * 2,
        scratch_shapes=[pltpu.VMEM((2, SIDE, width), jnp.float32)],
        compiler_params=limits(8),
        cost_estimate=cost(1 << 20, 1 << 25),
        name="columns_out",
    )(w_out, gains, sides, far_row, near_row)
    far_column, near_column = swap(*sent, "sy")

    (
        end_sum, end_part, four_sum, two_part, two_x, mid, rim_rows, ring_rows, rim_x,
    ) = pl.pallas_call(
        functools.partial(prepare, sizes, degree),
        out_shape=(
            halves,
            halves,
            like((4 * EAST, width), jnp.float32),
            halves,
            halves,
            like((OWN, variables), jnp.float32),
            like((4 * NORTH, width)),
            like((2 * NORTH, ALL)),
            like((2 * NORTH, width), jnp.float32),
        ),
        in_specs=[vmem] * 11 + [pl.BlockSpec(memory_space=pl.ANY)],
        out_specs=(vmem,) * 9,
        scratch_shapes=[
            pltpu.VMEM((OWN + 2 * NORTH, width), jnp.bfloat16),
            pltpu.VMEM((OWN + 2 * NORTH, width), jnp.float32),
            pltpu.VMEM((ALL - OWN, width), jnp.bfloat16),
            pltpu.VMEM((OWN, width), jnp.float32),
        ],
        compiler_params=limits(16),
        cost_estimate=cost(1 << 24, 1 << 25),
        name="prepare",
    )(
        x, first, gains, links, own_sum, w_self, w_nbr, w_out, w_dec, far_row, near_row, sent[1]
    )

    busy = 2 * EAST + OUT - OWN
    preds, shares, _ = pl.pallas_call(
        functools.partial(advance, sizes, degree),
        out_shape=(like((OWN, variables)),) * 2 + (like(mid.shape, jnp.float32),),
        in_specs=[vmem] * 19,
        out_specs=(vmem,) * 3,
        input_output_aliases={8: 2},
        scratch_shapes=[
            pltpu.VMEM((ALL - OWN, width), jnp.bfloat16),
            pltpu.VMEM((2 * LANES, width), jnp.bfloat16),
            pltpu.VMEM((busy, width), jnp.bfloat16),
            pltpu.VMEM((busy, width), jnp.float32),
            pltpu.VMEM((OUT - OWN, ALL), jnp.bfloat16),
        ],
        compiler_params=limits(16),
        cost_estimate=cost(1 << 31, 1 << 23),
        name="advance",
    )(
        first, gains, four_links, end_sum, end_part, four_sum, two_part, two_x, mid,
        rim_rows, ring_rows, rim_x, sides, far_column, near_column, w_self, w_nbr, w_out, w_dec,
    )

    members = lax.axis_size("member")
    share = OWN // members
    mine = lax.all_to_all(shares.reshape(members, share, variables), "member", 0, 0)
    copies = pl.pallas_call(
        score_share,
        out_shape=like(mine.shape),
        in_specs=[vmem] * 2,
        out_specs=vmem,
        compiler_params=limits(8),
        name="score_share",
    )(mine, target.reshape(OWN, variables))
    scores = lax.all_to_all(copies, "member", 0, 0).astype(jnp.float32)
    return (preds.reshape(1, EAST, NORTH, variables), scores.reshape(target.shape))


def solution(mesh):
    placed = (
        P("member", "sx", "sy", None),
        P("member", None),
        P("sx", "sy", None),
        P("sx", "sy", None),
        P(),
        P(),
        P(),
        P(),
        P(),
        P(),
    )
    return jax.shard_map(
        local,
        mesh=mesh,
        in_specs=placed,
        out_specs=(P("member", "sx", "sy", None), P("sx", "sy", None)),
        check_vma=False,
    )
```

```python
import functools

import jax
import jax.numpy as jnp
from jax import lax
from jax.experimental import pallas as pl
from jax.experimental.pallas import tpu as pltpu
from jax.sharding import PartitionSpec as P

EAST = 32
NORTH = 16
OWN = EAST * NORTH
LONG = EAST + 4
PAD = 48
CODED = 40
FAR = 56
SIDE = 96
LANES = 128
CODE = 1024
OUT = OWN + 2 * NORTH + 2 * PAD
ALL = OUT + 2 * NORTH + 2 * PAD
EPS = 1e-05


def place(row, column):
    inner = jnp.where(
        (row >= 0) & (row < EAST),
        row * NORTH + column,
        jnp.where(
            row == -1,
            OWN + column,
            jnp.where(
                row == EAST,
                OWN + NORTH + column,
                jnp.where(row == -2, OUT + column, OUT + NORTH + column),
            ),
        ),
    )
    side = jnp.where(
        column == -1,
        OWN + 2 * NORTH,
        jnp.where(
            column == NORTH,
            OWN + 2 * NORTH + PAD,
            jnp.where(column == -2, OUT + 2 * NORTH, OUT + 2 * NORTH + PAD),
        ),
    )
    return jnp.where((column >= 0) & (column < NORTH), inner, side + row + 2)


def neighbours(codes, row, column, spot, sizes):
    third = (codes >= 3).astype(jnp.int32) + (codes >= 6).astype(jnp.int32)
    to_row = row + third - 1
    to_column = column + (codes - 3 * third) - 1
    east = spot[0] * EAST + to_row
    north = spot[1] * NORTH + to_column
    real = (east >= 0) & (east < sizes[0]) & (north >= 0) & (north < sizes[1])
    real = real & (row >= -1) & (row <= EAST)
    return jnp.where(real, place(to_row, to_column), -1)


def counted(slots, at, width):
    lanes = lax.broadcasted_iota(jnp.int32, (slots[0].shape[0], width), 1) + at
    total = jnp.zeros(lanes.shape, jnp.float32)
    for slot in slots:
        total = total + jnp.where(lanes == slot, 1.0, 0.0)
    return total.astype(jnp.bfloat16)


def apart(index, degree):
    return [index[:, slot : slot + 1] for slot in range(degree)]


def norm(x):
    away = x - jnp.mean(x, axis=-1, keepdims=True)
    var = jnp.mean(away * away, axis=-1, keepdims=True)
    return away * lax.rsqrt(var + EPS)


def dot(a, b):
    return jnp.dot(a, b, preferred_element_type=jnp.float32)


def here(axis):
    return lax.axis_index(axis).astype(jnp.int32)


def rows_out(degree, top, bottom, codes, far_out, near_out):
    lane = lax.broadcasted_iota(jnp.int32, (NORTH, LANES), 1)
    lines = []
    for row in (0, EAST - 1):
        named = jnp.zeros((NORTH, LANES), jnp.int32)
        for slot in range(degree):
            named = jnp.where(lane == slot, codes[slot, :, row : row + 1], named)
        lines.append(named.astype(jnp.float32).astype(jnp.bfloat16))
    odd = here("sx") % 2 == 1
    for out, is_top in ((far_out, jnp.logical_not(odd)), (near_out, odd)):
        out[: 2 * NORTH] = jnp.where(is_top, top[...], bottom[...])
        out[2 * NORTH :] = jnp.zeros((NORTH, out.shape[1]), jnp.bfloat16)
        out[2 * NORTH :, :LANES] = jnp.where(is_top, lines[0], lines[1])


def hand_on(message, *others):
    out = others[-1]
    out[...] = message[...]


def sorted_by(axis, far, near):
    odd = here(axis) % 2 == 1
    far, near = (far[...].astype(jnp.float32), near[...].astype(jnp.float32))
    return jnp.where(odd, near, far), jnp.where(odd, far, near)


def by_row(slots, column, turned):
    turned[...] = jnp.zeros(turned.shape, jnp.float32)
    for slot in range(slots.shape[0]):
        turned[slot : slot + 1, :EAST] = slots[slot, column : column + 1].astype(jnp.float32)
    return turned[...].T[:EAST]


def collect(degree, x, coded, sides, named):
    sides[...] = jnp.zeros(sides.shape, jnp.float32)
    named[...] = jnp.zeros(named.shape, jnp.float32)
    lines = 8
    rows = lines * NORTH
    for part in range(EAST // lines):
        span = slice(part * rows, (part + 1) * rows)
        grid = x[span].astype(jnp.float32).reshape(lines, NORTH, x.shape[1])
        held = coded[span].reshape(lines, NORTH, degree)
        at = 2 + part * lines
        for side, (near, far) in enumerate(((0, 1), (NORTH - 1, NORTH - 2))):
            sides[side, at : at + lines] = grid[:, near]
            sides[side, FAR + at : FAR + at + lines] = grid[:, far]
            named[side, at : at + lines, :degree] = (held[:, near] & (CODE - 1)).astype(jnp.float32)
    for side in range(2):
        for part in range(PAD // 16):
            sides[side, CODED:FAR, part * LANES : (part + 1) * LANES] = named[
                side, part * 16 : (part + 1) * 16
            ]


def active(v, gains, layer):
    return norm(v) * gains[2 * layer : 2 * layer + 1] + gains[2 * layer + 1 : 2 * layer + 2]


def rest(total, part, w_nbr, w_out, layer):
    hidden = jax.nn.silu(part + dot(total, w_nbr[layer])).astype(jnp.bfloat16)
    return dot(hidden, w_out[layer])


def ends(v):
    grid = v.reshape(EAST, NORTH, v.shape[-1])
    return jnp.concatenate([grid[:, 0], grid[:, NORTH - 1]], axis=0)


FOUR = (0, NORTH - 1, 1, NORTH - 2)


def begin(
    sizes, x, slots, noise, w_scale, w_shift, first, gains, links, four_links, own_sum,
    index, turned,
):
    degree = slots.shape[0]
    for layer in range(w_scale.shape[0]):
        for at, w in enumerate((w_scale, w_shift)):
            gains[2 * layer + at : 2 * layer + at + 1] = (1.0 - at) + jnp.dot(
                noise[...], w[layer], precision=lax.Precision.HIGHEST,
                preferred_element_type=jnp.float32,
            )
    links[...] = jnp.zeros(links.shape, jnp.bfloat16)
    first[...] = active(x[...].astype(jnp.float32), gains, 0).astype(jnp.bfloat16)
    found = neighbours(
        slots[...],
        lax.broadcasted_iota(jnp.int32, slots.shape, 2),
        lax.broadcasted_iota(jnp.int32, slots.shape, 1),
        (here("sx"), here("sy")),
        sizes,
    )
    index[0] = found
    line, step = (found // NORTH, found % NORTH)
    end = jnp.where(step == 0, line, jnp.where(step == NORTH - 1, EAST + line, -1))
    index[1] = jnp.where((found >= 0) & (found < OWN), end, -1)
    for row in range(EAST):
        span = slice(row * NORTH, (row + 1) * NORTH)
        named = [index[0, slot, :, row : row + 1] for slot in range(degree)]
        tiles = {max(row - 1, 0) * NORTH // LANES, min(row + 1, EAST - 1) * NORTH // LANES}
        for tile in sorted(tiles) + [OWN // LANES]:
            links[span, tile * LANES : (tile + 1) * LANES] = counted(named, tile * LANES, LANES)
    for part, column in enumerate(FOUR):
        for which, at in enumerate((OWN, 0)):
            turn = by_row(index.at[which], column, turned.at[2 * part + which])
            four_links[part * EAST : (part + 1) * EAST, which * LANES : (which + 1) * LANES] = (
                counted(apart(turn.astype(jnp.int32), degree), at, LANES)
            )
    own_sum[...] = dot(links[:, :OWN], first[...])


def own_neighbours(arrived, row0, column0, sizes, degree):
    if column0 == 0:
        held = arrived[2 * NORTH : 3 * NORTH, :LANES]
    else:
        held = jnp.concatenate(
            [arrived[CODED:FAR, i * LANES : (i + 1) * LANES] for i in range(PAD // 16)], axis=0
        )
    held = held[:, :degree].astype(jnp.int32)
    step = lax.broadcasted_iota(jnp.int32, held.shape, 0)
    if column0 == 0:
        row, column = (jnp.full(held.shape, row0, jnp.int32), step)
    else:
        row, column = (row0 + step, jnp.full(held.shape, column0, jnp.int32))
    index = neighbours(held, row, column, (here("sx"), here("sy")), sizes)
    return counted(apart(index, degree), 0, ALL)


def columns(v, which):
    grid = v.reshape(EAST, NORTH, v.shape[-1])
    return jnp.concatenate([grid[:, column] for column in which], axis=0)


def prepare(
    sizes, degree, x, first, gains, links, own_sum, w_self, w_nbr, w_out, w_dec,
    far_row, near_row, sent,
    end_sum, end_part, four_sum, two_part, two_x, mid, rim_rows, ring_rows, rim_x,
    total, part, rim, state,
):
    sixth = 1.0 / degree
    own = slice(0, OWN)
    top, bottom = sorted_by("sx", far_row, near_row)
    nearer = jnp.concatenate([top[NORTH : 2 * NORTH], bottom[:NORTH]], axis=0)
    rows = 2 * NORTH
    rim_x[...] = nearer
    rim_rows[:rows] = active(nearer, gains, 0).astype(jnp.bfloat16)
    rim_rows[rows:] = active(
        jnp.concatenate([top[:NORTH], bottom[NORTH : 2 * NORTH]], axis=0), gains, 0
    ).astype(jnp.bfloat16)
    rim[...] = jnp.zeros(rim.shape, jnp.bfloat16)
    rim[:rows] = rim_rows[:rows]
    rim[OUT - OWN : OUT - OWN + rows] = rim_rows[rows:]
    ring_rows[:NORTH] = own_neighbours(top, -1, 0, sizes, degree)
    ring_rows[NORTH:] = own_neighbours(bottom, EAST, 0, sizes, degree)

    part[own] = dot(first[...], w_self[0])
    end_part[...] = ends(part[own])
    end_sum[...] = ends(own_sum[...])
    part[OWN:] = dot(rim_rows[:rows], w_self[0])
    total[own] = (
        (own_sum[...] + dot(links[:, OWN:], rim[: OUT - OWN])) * sixth
    ).astype(jnp.bfloat16)
    total[OWN:] = (
        (dot(ring_rows[:, :OWN], first[...]) + dot(ring_rows[:, OWN:], rim[...])) * sixth
    ).astype(jnp.bfloat16)
    step = lax.broadcasted_iota(jnp.int32, (OWN // 2, 1), 0) % NORTH
    inner = (step > 0) & (step < NORTH - 1)
    spans = [slice(0, OWN // 2), slice(OWN // 2, OWN + rows)]
    ready = [part[span] + dot(total[span], w_nbr[0]) for span in spans]
    done = [dot(jax.nn.silu(v).astype(jnp.bfloat16), w_out[0]) for v in ready]
    rim[:rows] = active(nearer + done[1][OWN // 2 :], gains, 1).astype(jnp.bfloat16)
    held = []
    for at, v in zip((0, OWN // 2), done):
        span = slice(at, at + OWN // 2)
        state[span] = x[span].astype(jnp.float32) + v[: OWN // 2]
        held.append(jnp.where(inner, active(state[span], gains, 1), 0.0).astype(jnp.bfloat16))
    a1 = jnp.concatenate(held, axis=0)
    two_x[...] = columns(state[...], FOUR[2:])
    sums = dot(links[:, :OWN], a1)
    four_sum[...] = columns(sums, FOUR)
    part[own] = dot(a1, w_self[1])
    two_part[...] = columns(part[own], FOUR[2:])
    halves = [slice(0, OWN // 2), slice(OWN // 2, OWN)]
    ready = []
    for span in halves:
        mixed = (sums[span] + dot(links[span, OWN:], rim[: OUT - OWN])) * sixth
        ready.append(part[span] + dot(mixed.astype(jnp.bfloat16), w_nbr[1]))
    done = []
    for span, v in zip(halves, ready):
        hidden = jax.nn.silu(v).astype(jnp.bfloat16)
        done.append(state[span] + dot(hidden, w_out[1]))
    for span, v in zip(halves, done):
        mid[span] = dot(norm(v).astype(jnp.bfloat16), w_dec[...])


def columns_out(w_out, gains, sides, far_row, near_row, far_out, near_out, lines):
    top, bottom = sorted_by("sx", far_row, near_row)
    for side, (near, far) in enumerate(((0, 1), (NORTH - 1, NORTH - 2))):
        lines[side] = sides[side]
        for at, column in ((0, near), (FAR, far)):
            for step, source, row in (
                (0, top, 0), (1, top, 1), (EAST + 2, bottom, 0), (EAST + 3, bottom, 1)
            ):
                picked = row * NORTH + column
                lines[side, at + step : at + step + 1] = source[picked : picked + 1]
        picked = 2 * NORTH + near
        lines[side, CODED + 1 : CODED + 2, :LANES] = top[picked : picked + 1, :LANES]
        part, line = divmod(EAST + 2, 16)
        lines[side, CODED + line : CODED + line + 1, part * LANES : (part + 1) * LANES] = bottom[
            picked : picked + 1, :LANES
        ]
    odd = here("sy") % 2
    far_out[...] = lines[odd].astype(jnp.bfloat16)
    near_out[...] = lines[1 - odd].astype(jnp.bfloat16)


def advance(
    sizes, degree, first, gains, four_links, end_sum, end_part, four_sum, two_part, two_x, old_mid,
    rim_rows, ring_rows, rim_x, sides, far_column, near_column, w_self, w_nbr, w_out, w_dec,
    preds, sent, mid, rim_first, late, total, part, ring,
):
    sixth = 1.0 / degree
    west, east = sorted_by("sy", far_column, near_column)
    nearer = jnp.concatenate([west[:PAD], east[:PAD]], axis=0)
    gap = jnp.zeros((PAD - SIDE + FAR, west.shape[1]), jnp.float32)
    farther = jnp.concatenate([west[FAR:], gap, east[FAR:], gap], axis=0)
    near = slice(0, OUT - OWN)
    rows = 2 * NORTH
    rim_first[:rows] = rim_rows[:rows]
    rim_first[rows : OUT - OWN] = active(nearer, gains, 0).astype(jnp.bfloat16)
    rim_first[OUT - OWN : OUT - OWN + rows] = rim_rows[rows:]
    rim_first[OUT - OWN + rows :] = active(farther, gains, 0).astype(jnp.bfloat16)
    ring[:rows] = ring_rows[...]
    ring[rows : rows + PAD] = own_neighbours(west, -2, -1, sizes, degree)
    ring[rows + PAD :] = own_neighbours(east, -2, NORTH, sizes, degree)

    ended = slice(0, 2 * EAST)
    total[ended] = ((end_sum[...] + dot(four_links[ended, :LANES], rim_first[near])) * sixth).astype(jnp.bfloat16)
    total[2 * EAST :] = (
        (dot(ring[:, :OWN], first[...]) + dot(ring[:, OWN:], rim_first[...])) * sixth
    ).astype(jnp.bfloat16)
    part[ended] = end_part[...]
    part[2 * EAST :] = dot(rim_first[near], w_self[0])
    v = rest(total[...], part[...], w_nbr, w_out, 0)
    column = slice(2, 2 + EAST)
    v_ends = v[ended] + jnp.concatenate([sides[0, column], sides[1, column]], axis=0)
    v_ring = v[2 * EAST :] + jnp.concatenate([rim_x[...], nearer], axis=0)
    a_ends = active(v_ends, gains, 1).astype(jnp.bfloat16)
    late[near] = active(v_ring, gains, 1).astype(jnp.bfloat16)
    late[OUT - OWN : OUT - OWN + 2 * EAST] = a_ends
    late[OUT - OWN + 2 * EAST :] = jnp.zeros((LANES - 2 * EAST, late.shape[1]), jnp.bfloat16)

    sums = ((four_sum[...] + dot(four_links[...], late[...])) * sixth).astype(jnp.bfloat16)
    own_part = jnp.concatenate([dot(a_ends, w_self[1]), two_part[...]], axis=0)
    v = jnp.concatenate([v_ends, two_x[...]], axis=0) + rest(sums, own_part, w_nbr, w_out, 1)
    value = dot(norm(v).astype(jnp.bfloat16), w_dec[...])
    for at, place_in in enumerate(FOUR):
        mid[pl.ds(place_in, EAST, stride=NORTH)] = value[at * EAST : (at + 1) * EAST]
    value = mid[...].astype(jnp.bfloat16)
    preds[...] = value
    sent[...] = value


def score_share(mine, truth, copies):
    members, share, _ = mine.shape
    denom = 2.0 * members * (members - 1)
    held = [mine[one].astype(jnp.float32) for one in range(members)]
    goal = truth[pl.ds(pl.multiple_of(here("member") * share, share), share)].astype(jnp.float32)
    skill = jnp.zeros(goal.shape, jnp.float32)
    spread = jnp.zeros(goal.shape, jnp.float32)
    for one in range(members):
        skill = skill + jnp.abs(held[one] - goal)
        for two in range(one):
            spread = spread + jnp.abs(held[one] - held[two])
    score = (skill * (1.0 / members) - spread * (2.0 / denom)).astype(jnp.bfloat16)
    for one in range(members):
        copies[one] = score


def swap(far, near, axis):
    peers = lax.axis_size(axis)
    pairs = [[(i, i + 1), (i + 1, i)] for i in range(peers - 1)]
    from_near = lax.ppermute(near, axis, sum(pairs[0::2], []))
    return lax.ppermute(far, axis, sum(pairs[1::2], [])), from_near


def local(states, noises, codes, target, w_self, w_nbr, w_out, w_scale, w_shift, w_dec):
    width = states.shape[-1]
    degree = codes.shape[-1]
    variables = w_dec.shape[-1]
    layers = w_self.shape[0]
    x = states.reshape(OWN, width)
    sizes = (lax.axis_size("sx") * EAST, lax.axis_size("sy") * NORTH)
    vmem = pl.BlockSpec(memory_space=pltpu.VMEM)

    def like(shape, dtype=jnp.bfloat16):
        return jax.ShapeDtypeStruct(shape, dtype)

    def limits(mib):
        return pltpu.CompilerParams(vmem_limit_bytes=mib << 20)

    def cost(flops, size):
        return pl.CostEstimate(flops=flops, bytes_accessed=size, transcendentals=0)

    slots = codes.transpose(2, 1, 0)
    far_out, near_out = (
        pl.pallas_call(
            functools.partial(rows_out, degree),
            grid=(1,),
            out_shape=(like((3 * NORTH, width)),) * 2,
            in_specs=[
                pl.BlockSpec((2 * NORTH, width), lambda i: (0, 0)),
                pl.BlockSpec((2 * NORTH, width), lambda i: (OWN // (2 * NORTH) - 1, 0)),
                pl.BlockSpec(slots.shape, lambda i: (0, 0, 0)),
            ],
            out_specs=(pl.BlockSpec((3 * NORTH, width), lambda i: (0, 0)),) * 2,
            compiler_params=pltpu.CompilerParams(vmem_limit_bytes=55104 << 10),
            name="rows_out",
        )(x, x, slots)
    )
    far_out = pl.pallas_call(
        hand_on,
        out_shape=like(far_out.shape),
        in_specs=[vmem] + [pl.BlockSpec(memory_space=pl.ANY)] * 4,
        out_specs=vmem,
        compiler_params=limits(8),
        name="hand_on",
    )(far_out, near_out, noises, w_scale, w_shift)
    far_row, near_row = swap(far_out, near_out, "sx")

    coded = (slots + CODE * here("sx")).transpose(2, 1, 0).reshape(OWN, degree)
    sides = pl.pallas_call(
        functools.partial(collect, degree),
        out_shape=like((2, SIDE, width), jnp.float32),
        in_specs=[vmem] * 2,
        out_specs=vmem,
        scratch_shapes=[pltpu.VMEM((2, PAD, LANES), jnp.float32)],
        compiler_params=limits(8),
        cost_estimate=cost(1 << 20, 1 << 25),
        name="collect",
    )(x, coded)

    wide = like((OWN, width), jnp.float32)
    halves = like((2 * EAST, width), jnp.float32)
    first, gains, links, four_links, own_sum = pl.pallas_call(
        functools.partial(begin, sizes),
        out_shape=(
            like((OWN, width)),
            like((2 * layers, width), jnp.float32),
            like((OWN, OUT)),
            like((4 * EAST, 2 * LANES)),
            wide,
        ),
        in_specs=[vmem] * 5,
        out_specs=(vmem,) * 5,
        scratch_shapes=[
            pltpu.VMEM((2,) + slots.shape, jnp.int32),
            pltpu.VMEM((8, 8, LANES), jnp.float32),
        ],
        compiler_params=limits(8),
        cost_estimate=cost(1 << 24, 1 << 24),
        name="begin",
    )(x, slots, noises, w_scale, w_shift)

    sent = pl.pallas_call(
        columns_out,
        out_shape=(like((SIDE, width)),) * 2,
        in_specs=[pl.BlockSpec(memory_space=pl.ANY)] * 2 + [vmem] * 3,
        out_specs=(vmem,) * 2,
        scratch_shapes=[pltpu.VMEM((2, SIDE, width), jnp.float32)],
        compiler_params=limits(8),
        cost_estimate=cost(1 << 20, 1 << 25),
        name="columns_out",
    )(w_out, gains, sides, far_row, near_row)
    far_column, near_column = swap(*sent, "sy")

    (
        end_sum, end_part, four_sum, two_part, two_x, mid, rim_rows, ring_rows, rim_x,
    ) = pl.pallas_call(
        functools.partial(prepare, sizes, degree),
        out_shape=(
            halves,
            halves,
            like((4 * EAST, width), jnp.float32),
            halves,
            halves,
            like((OWN, variables), jnp.float32),
            like((4 * NORTH, width)),
            like((2 * NORTH, ALL)),
            like((2 * NORTH, width), jnp.float32),
        ),
        in_specs=[vmem] * 11 + [pl.BlockSpec(memory_space=pl.ANY)],
        out_specs=(vmem,) * 9,
        scratch_shapes=[
            pltpu.VMEM((OWN + 2 * NORTH, width), jnp.bfloat16),
            pltpu.VMEM((OWN + 2 * NORTH, width), jnp.float32),
            pltpu.VMEM((ALL - OWN, width), jnp.bfloat16),
            pltpu.VMEM((OWN, width), jnp.float32),
        ],
        compiler_params=limits(16),
        cost_estimate=cost(1 << 24, 1 << 25),
        name="prepare",
    )(
        x, first, gains, links, own_sum, w_self, w_nbr, w_out, w_dec, far_row, near_row, sent[1]
    )

    busy = 2 * EAST + OUT - OWN
    preds, shares, _ = pl.pallas_call(
        functools.partial(advance, sizes, degree),
        out_shape=(like((OWN, variables)),) * 2 + (like(mid.shape, jnp.float32),),
        in_specs=[vmem] * 19,
        out_specs=(vmem,) * 3,
        input_output_aliases={8: 2},
        scratch_shapes=[
            pltpu.VMEM((ALL - OWN, width), jnp.bfloat16),
            pltpu.VMEM((2 * LANES, width), jnp.bfloat16),
            pltpu.VMEM((busy, width), jnp.bfloat16),
            pltpu.VMEM((busy, width), jnp.float32),
            pltpu.VMEM((OUT - OWN, ALL), jnp.bfloat16),
        ],
        compiler_params=limits(16),
        cost_estimate=cost(1 << 31, 1 << 23),
        name="advance",
    )(
        first, gains, four_links, end_sum, end_part, four_sum, two_part, two_x, mid,
        rim_rows, ring_rows, rim_x, sides, far_column, near_column, w_self, w_nbr, w_out, w_dec,
    )

    members = lax.axis_size("member")
    share = OWN // members
    mine = lax.all_to_all(shares.reshape(members, share, variables), "member", 0, 0)
    copies = pl.pallas_call(
        score_share,
        out_shape=like(mine.shape),
        in_specs=[vmem] * 2,
        out_specs=vmem,
        compiler_params=limits(8),
        name="score_share",
    )(mine, target.reshape(OWN, variables))
    scores = lax.all_to_all(copies, "member", 0, 0).astype(jnp.float32)
    return (preds.reshape(1, EAST, NORTH, variables), scores.reshape(target.shape))


def solution(mesh):
    placed = (
        P("member", "sx", "sy", None),
        P("member", None),
        P("sx", "sy", None),
        P("sx", "sy", None),
        P(),
        P(),
        P(),
        P(),
        P(),
        P(),
    )
    return jax.shard_map(
        local,
        mesh=mesh,
        in_specs=placed,
        out_specs=(P("member", "sx", "sy", None), P("sx", "sy", None)),
        check_vma=False,
    )
```

```python
import functools

import jax
import jax.numpy as jnp
from jax import lax
from jax.experimental import pallas as pl
from jax.experimental.pallas import tpu as pltpu
from jax.sharding import PartitionSpec as P

EAST = 32
NORTH = 16
OWN = EAST * NORTH
LONG = EAST + 4
PAD = 48
CODED = 40
FAR = 56
SIDE = 96
LANES = 128
CODE = 1024
OUT = OWN + 2 * NORTH + 2 * PAD
ALL = OUT + 2 * NORTH + 2 * PAD
EPS = 1e-05


def place(row, column):
    inner = jnp.where(
        (row >= 0) & (row < EAST),
        row * NORTH + column,
        jnp.where(
            row == -1,
            OWN + column,
            jnp.where(
                row == EAST,
                OWN + NORTH + column,
                jnp.where(row == -2, OUT + column, OUT + NORTH + column),
            ),
        ),
    )
    side = jnp.where(
        column == -1,
        OWN + 2 * NORTH,
        jnp.where(
            column == NORTH,
            OWN + 2 * NORTH + PAD,
            jnp.where(column == -2, OUT + 2 * NORTH, OUT + 2 * NORTH + PAD),
        ),
    )
    return jnp.where((column >= 0) & (column < NORTH), inner, side + row + 2)


def neighbours(codes, row, column, spot, sizes):
    third = (codes >= 3).astype(jnp.int32) + (codes >= 6).astype(jnp.int32)
    to_row = row + third - 1
    to_column = column + (codes - 3 * third) - 1
    east = spot[0] * EAST + to_row
    north = spot[1] * NORTH + to_column
    real = (east >= 0) & (east < sizes[0]) & (north >= 0) & (north < sizes[1])
    real = real & (row >= -1) & (row <= EAST)
    return jnp.where(real, place(to_row, to_column), -1)


def counted(slots, at, width):
    lanes = lax.broadcasted_iota(jnp.int32, (slots[0].shape[0], width), 1) + at
    total = jnp.zeros(lanes.shape, jnp.float32)
    for slot in slots:
        total = total + jnp.where(lanes == slot, 1.0, 0.0)
    return total.astype(jnp.bfloat16)


def apart(index, degree):
    return [index[:, slot : slot + 1] for slot in range(degree)]


def norm(x):
    away = x - jnp.mean(x, axis=-1, keepdims=True)
    var = jnp.mean(away * away, axis=-1, keepdims=True)
    return away * lax.rsqrt(var + EPS)


def dot(a, b):
    return jnp.dot(a, b, preferred_element_type=jnp.float32)


def here(axis):
    return lax.axis_index(axis).astype(jnp.int32)


def rows_out(degree, top, bottom, codes, far_out, near_out):
    lane = lax.broadcasted_iota(jnp.int32, (NORTH, LANES), 1)
    lines = []
    for row in (0, EAST - 1):
        named = jnp.zeros((NORTH, LANES), jnp.int32)
        for slot in range(degree):
            named = jnp.where(lane == slot, codes[slot, :, row : row + 1], named)
        lines.append(named.astype(jnp.float32).astype(jnp.bfloat16))
    odd = here("sx") % 2 == 1
    for out, is_top in ((far_out, jnp.logical_not(odd)), (near_out, odd)):
        out[: 2 * NORTH] = jnp.where(is_top, top[...], bottom[...])
        out[2 * NORTH :] = jnp.zeros((NORTH, out.shape[1]), jnp.bfloat16)
        out[2 * NORTH :, :LANES] = jnp.where(is_top, lines[0], lines[1])


def hand_on(message, *others):
    out = others[-1]
    out[...] = message[...]


def sorted_by(axis, far, near):
    odd = here(axis) % 2 == 1
    far, near = (far[...].astype(jnp.float32), near[...].astype(jnp.float32))
    return jnp.where(odd, near, far), jnp.where(odd, far, near)


def by_row(slots, column, turned):
    turned[...] = jnp.zeros(turned.shape, jnp.float32)
    for slot in range(slots.shape[0]):
        turned[slot : slot + 1, :EAST] = slots[slot, column : column + 1].astype(jnp.float32)
    return turned[...].T[:EAST]


def collect(degree, x, coded, sides, named):
    sides[...] = jnp.zeros(sides.shape, jnp.float32)
    named[...] = jnp.zeros(named.shape, jnp.float32)
    lines = 8
    rows = lines * NORTH
    for part in range(EAST // lines):
        span = slice(part * rows, (part + 1) * rows)
        grid = x[span].astype(jnp.float32).reshape(lines, NORTH, x.shape[1])
        held = coded[span].reshape(lines, NORTH, degree)
        at = 2 + part * lines
        for side, (near, far) in enumerate(((0, 1), (NORTH - 1, NORTH - 2))):
            sides[side, at : at + lines] = grid[:, near]
            sides[side, FAR + at : FAR + at + lines] = grid[:, far]
            named[side, at : at + lines, :degree] = (held[:, near] & (CODE - 1)).astype(jnp.float32)
    for side in range(2):
        for part in range(PAD // 16):
            sides[side, CODED:FAR, part * LANES : (part + 1) * LANES] = named[
                side, part * 16 : (part + 1) * 16
            ]


def active(v, gains, layer):
    return norm(v) * gains[2 * layer : 2 * layer + 1] + gains[2 * layer + 1 : 2 * layer + 2]


def rest(total, part, w_nbr, w_out, layer):
    hidden = jax.nn.silu(part + dot(total, w_nbr[layer])).astype(jnp.bfloat16)
    return dot(hidden, w_out[layer])


def ends(v):
    grid = v.reshape(EAST, NORTH, v.shape[-1])
    return jnp.concatenate([grid[:, 0], grid[:, NORTH - 1]], axis=0)


FOUR = (0, NORTH - 1, 1, NORTH - 2)


def begin(
    sizes, x, slots, noise, w_scale, w_shift, first, gains, links, four_links, own_sum,
    index, turned,
):
    degree = slots.shape[0]
    for layer in range(w_scale.shape[0]):
        for at, w in enumerate((w_scale, w_shift)):
            gains[2 * layer + at : 2 * layer + at + 1] = (1.0 - at) + jnp.dot(
                noise[...], w[layer], precision=lax.Precision.HIGHEST,
                preferred_element_type=jnp.float32,
            )
    links[...] = jnp.zeros(links.shape, jnp.bfloat16)
    first[...] = active(x[...].astype(jnp.float32), gains, 0).astype(jnp.bfloat16)
    found = neighbours(
        slots[...],
        lax.broadcasted_iota(jnp.int32, slots.shape, 2),
        lax.broadcasted_iota(jnp.int32, slots.shape, 1),
        (here("sx"), here("sy")),
        sizes,
    )
    index[0] = found
    line, step = (found // NORTH, found % NORTH)
    end = jnp.where(step == 0, line, jnp.where(step == NORTH - 1, EAST + line, -1))
    index[1] = jnp.where((found >= 0) & (found < OWN), end, -1)
    for row in range(EAST):
        span = slice(row * NORTH, (row + 1) * NORTH)
        named = [index[0, slot, :, row : row + 1] for slot in range(degree)]
        tiles = {max(row - 1, 0) * NORTH // LANES, min(row + 1, EAST - 1) * NORTH // LANES}
        for tile in sorted(tiles) + [OWN // LANES]:
            links[span, tile * LANES : (tile + 1) * LANES] = counted(named, tile * LANES, LANES)
    for part, column in enumerate(FOUR):
        for which, at in enumerate((OWN, 0)):
            turn = by_row(index.at[which], column, turned.at[2 * part + which])
            four_links[part * EAST : (part + 1) * EAST, which * LANES : (which + 1) * LANES] = (
                counted(apart(turn.astype(jnp.int32), degree), at, LANES)
            )
    own_sum[...] = dot(links[:, :OWN], first[...])


def own_neighbours(arrived, row0, column0, sizes, degree):
    if column0 == 0:
        held = arrived[2 * NORTH : 3 * NORTH, :LANES]
    else:
        held = jnp.concatenate(
            [arrived[CODED:FAR, i * LANES : (i + 1) * LANES] for i in range(PAD // 16)], axis=0
        )
    held = held[:, :degree].astype(jnp.int32)
    step = lax.broadcasted_iota(jnp.int32, held.shape, 0)
    if column0 == 0:
        row, column = (jnp.full(held.shape, row0, jnp.int32), step)
    else:
        row, column = (row0 + step, jnp.full(held.shape, column0, jnp.int32))
    index = neighbours(held, row, column, (here("sx"), here("sy")), sizes)
    return counted(apart(index, degree), 0, ALL)


def columns(v, which):
    grid = v.reshape(EAST, NORTH, v.shape[-1])
    return jnp.concatenate([grid[:, column] for column in which], axis=0)


def prepare(
    sizes, degree, x, first, gains, links, own_sum, w_self, w_nbr, w_out, w_dec,
    far_row, near_row, sent,
    end_sum, end_part, four_sum, two_part, two_x, mid, rim_rows, ring_rows, rim_x,
    total, part, rim, state,
):
    sixth = 1.0 / degree
    own = slice(0, OWN)
    top, bottom = sorted_by("sx", far_row, near_row)
    nearer = jnp.concatenate([top[NORTH : 2 * NORTH], bottom[:NORTH]], axis=0)
    rows = 2 * NORTH
    rim_x[...] = nearer
    rim_rows[:rows] = active(nearer, gains, 0).astype(jnp.bfloat16)
    rim_rows[rows:] = active(
        jnp.concatenate([top[:NORTH], bottom[NORTH : 2 * NORTH]], axis=0), gains, 0
    ).astype(jnp.bfloat16)
    rim[...] = jnp.zeros(rim.shape, jnp.bfloat16)
    rim[:rows] = rim_rows[:rows]
    rim[OUT - OWN : OUT - OWN + rows] = rim_rows[rows:]
    ring_rows[:NORTH] = own_neighbours(top, -1, 0, sizes, degree)
    ring_rows[NORTH:] = own_neighbours(bottom, EAST, 0, sizes, degree)

    part[own] = dot(first[...], w_self[0])
    end_part[...] = ends(part[own])
    end_sum[...] = ends(own_sum[...])
    part[OWN:] = dot(rim_rows[:rows], w_self[0])
    total[own] = (
        (own_sum[...] + dot(links[:, OWN:], rim[: OUT - OWN])) * sixth
    ).astype(jnp.bfloat16)
    total[OWN:] = (
        (
            dot(ring_rows[:, :LANES], first[:LANES])
            + dot(ring_rows[:, OWN - LANES : OWN], first[OWN - LANES :])
            + dot(ring_rows[:, OWN:], rim[...])
        )
        * sixth
    ).astype(jnp.bfloat16)
    step = lax.broadcasted_iota(jnp.int32, (OWN // 2, 1), 0) % NORTH
    inner = (step > 0) & (step < NORTH - 1)
    spans = [slice(0, OWN // 2), slice(OWN // 2, OWN + rows)]
    ready = [part[span] + dot(total[span], w_nbr[0]) for span in spans]
    done = [dot(jax.nn.silu(v).astype(jnp.bfloat16), w_out[0]) for v in ready]
    rim[:rows] = active(nearer + done[1][OWN // 2 :], gains, 1).astype(jnp.bfloat16)
    held = []
    for at, v in zip((0, OWN // 2), done):
        span = slice(at, at + OWN // 2)
        state[span] = x[span].astype(jnp.float32) + v[: OWN // 2]
        held.append(jnp.where(inner, active(state[span], gains, 1), 0.0).astype(jnp.bfloat16))
    a1 = jnp.concatenate(held, axis=0)
    two_x[...] = columns(state[...], FOUR[2:])
    sums = dot(links[:, :OWN], a1)
    four_sum[...] = columns(sums, FOUR)
    part[own] = dot(a1, w_self[1])
    two_part[...] = columns(part[own], FOUR[2:])
    halves = [slice(0, OWN // 2), slice(OWN // 2, OWN)]
    ready = []
    for span in halves:
        mixed = (sums[span] + dot(links[span, OWN:], rim[: OUT - OWN])) * sixth
        ready.append(part[span] + dot(mixed.astype(jnp.bfloat16), w_nbr[1]))
    done = []
    for span, v in zip(halves, ready):
        hidden = jax.nn.silu(v).astype(jnp.bfloat16)
        done.append(state[span] + dot(hidden, w_out[1]))
    for span, v in zip(halves, done):
        mid[span] = dot(norm(v).astype(jnp.bfloat16), w_dec[...])


def columns_out(w_out, gains, sides, far_row, near_row, far_out, near_out, lines):
    top, bottom = sorted_by("sx", far_row, near_row)
    for side, (near, far) in enumerate(((0, 1), (NORTH - 1, NORTH - 2))):
        lines[side] = sides[side]
        for at, column in ((0, near), (FAR, far)):
            for step, source, row in (
                (0, top, 0), (1, top, 1), (EAST + 2, bottom, 0), (EAST + 3, bottom, 1)
            ):
                picked = row * NORTH + column
                lines[side, at + step : at + step + 1] = source[picked : picked + 1]
        picked = 2 * NORTH + near
        lines[side, CODED + 1 : CODED + 2, :LANES] = top[picked : picked + 1, :LANES]
        part, line = divmod(EAST + 2, 16)
        lines[side, CODED + line : CODED + line + 1, part * LANES : (part + 1) * LANES] = bottom[
            picked : picked + 1, :LANES
        ]
    odd = here("sy") % 2
    far_out[...] = lines[odd].astype(jnp.bfloat16)
    near_out[...] = lines[1 - odd].astype(jnp.bfloat16)


def advance(
    sizes, degree, first, gains, four_links, end_sum, end_part, four_sum, two_part, two_x, old_mid,
    rim_rows, ring_rows, rim_x, sides, far_column, near_column, w_self, w_nbr, w_out, w_dec,
    preds, sent, mid, rim_first, late, total, part, ring,
):
    sixth = 1.0 / degree
    west, east = sorted_by("sy", far_column, near_column)
    nearer = jnp.concatenate([west[:PAD], east[:PAD]], axis=0)
    gap = jnp.zeros((PAD - SIDE + FAR, west.shape[1]), jnp.float32)
    farther = jnp.concatenate([west[FAR:], gap, east[FAR:], gap], axis=0)
    near = slice(0, OUT - OWN)
    rows = 2 * NORTH
    rim_first[:rows] = rim_rows[:rows]
    rim_first[rows : OUT - OWN] = active(nearer, gains, 0).astype(jnp.bfloat16)
    rim_first[OUT - OWN : OUT - OWN + rows] = rim_rows[rows:]
    rim_first[OUT - OWN + rows :] = active(farther, gains, 0).astype(jnp.bfloat16)
    ring[:rows] = ring_rows[...]
    ring[rows : rows + PAD] = own_neighbours(west, -2, -1, sizes, degree)
    ring[rows + PAD :] = own_neighbours(east, -2, NORTH, sizes, degree)

    ended = slice(0, 2 * EAST)
    total[ended] = ((end_sum[...] + dot(four_links[ended, :LANES], rim_first[near])) * sixth).astype(jnp.bfloat16)
    total[2 * EAST :] = (
        (dot(ring[:, :OWN], first[...]) + dot(ring[:, OWN:], rim_first[...])) * sixth
    ).astype(jnp.bfloat16)
    part[ended] = end_part[...]
    part[2 * EAST :] = dot(rim_first[near], w_self[0])
    v = rest(total[...], part[...], w_nbr, w_out, 0)
    column = slice(2, 2 + EAST)
    v_ends = v[ended] + jnp.concatenate([sides[0, column], sides[1, column]], axis=0)
    v_ring = v[2 * EAST :] + jnp.concatenate([rim_x[...], nearer], axis=0)
    a_ends = active(v_ends, gains, 1).astype(jnp.bfloat16)
    late[near] = active(v_ring, gains, 1).astype(jnp.bfloat16)
    late[OUT - OWN : OUT - OWN + 2 * EAST] = a_ends
    late[OUT - OWN + 2 * EAST :] = jnp.zeros((LANES - 2 * EAST, late.shape[1]), jnp.bfloat16)

    sums = ((four_sum[...] + dot(four_links[...], late[...])) * sixth).astype(jnp.bfloat16)
    own_part = jnp.concatenate([dot(a_ends, w_self[1]), two_part[...]], axis=0)
    v = jnp.concatenate([v_ends, two_x[...]], axis=0) + rest(sums, own_part, w_nbr, w_out, 1)
    value = dot(norm(v).astype(jnp.bfloat16), w_dec[...])
    for at, place_in in enumerate(FOUR):
        mid[pl.ds(place_in, EAST, stride=NORTH)] = value[at * EAST : (at + 1) * EAST]
    value = mid[...].astype(jnp.bfloat16)
    preds[...] = value
    sent[...] = value


def score_share(mine, truth, copies):
    members, share, _ = mine.shape
    denom = 2.0 * members * (members - 1)
    held = [mine[one].astype(jnp.float32) for one in range(members)]
    goal = truth[pl.ds(pl.multiple_of(here("member") * share, share), share)].astype(jnp.float32)
    skill = jnp.zeros(goal.shape, jnp.float32)
    spread = jnp.zeros(goal.shape, jnp.float32)
    for one in range(members):
        skill = skill + jnp.abs(held[one] - goal)
        for two in range(one):
            spread = spread + jnp.abs(held[one] - held[two])
    score = (skill * (1.0 / members) - spread * (2.0 / denom)).astype(jnp.bfloat16)
    for one in range(members):
        copies[one] = score


def swap(far, near, axis):
    peers = lax.axis_size(axis)
    pairs = [[(i, i + 1), (i + 1, i)] for i in range(peers - 1)]
    from_near = lax.ppermute(near, axis, sum(pairs[0::2], []))
    return lax.ppermute(far, axis, sum(pairs[1::2], [])), from_near


def local(states, noises, codes, target, w_self, w_nbr, w_out, w_scale, w_shift, w_dec):
    width = states.shape[-1]
    degree = codes.shape[-1]
    variables = w_dec.shape[-1]
    layers = w_self.shape[0]
    x = states.reshape(OWN, width)
    sizes = (lax.axis_size("sx") * EAST, lax.axis_size("sy") * NORTH)
    vmem = pl.BlockSpec(memory_space=pltpu.VMEM)

    def like(shape, dtype=jnp.bfloat16):
        return jax.ShapeDtypeStruct(shape, dtype)

    def limits(mib):
        return pltpu.CompilerParams(vmem_limit_bytes=mib << 20)

    def cost(flops, size):
        return pl.CostEstimate(flops=flops, bytes_accessed=size, transcendentals=0)

    slots = codes.transpose(2, 1, 0)
    far_out, near_out = (
        pl.pallas_call(
            functools.partial(rows_out, degree),
            grid=(1,),
            out_shape=(like((3 * NORTH, width)),) * 2,
            in_specs=[
                pl.BlockSpec((2 * NORTH, width), lambda i: (0, 0)),
                pl.BlockSpec((2 * NORTH, width), lambda i: (OWN // (2 * NORTH) - 1, 0)),
                pl.BlockSpec(slots.shape, lambda i: (0, 0, 0)),
            ],
            out_specs=(pl.BlockSpec((3 * NORTH, width), lambda i: (0, 0)),) * 2,
            compiler_params=pltpu.CompilerParams(vmem_limit_bytes=55104 << 10),
            name="rows_out",
        )(x, x, slots)
    )
    far_out = pl.pallas_call(
        hand_on,
        out_shape=like(far_out.shape),
        in_specs=[vmem] + [pl.BlockSpec(memory_space=pl.ANY)] * 4,
        out_specs=vmem,
        compiler_params=limits(8),
        name="hand_on",
    )(far_out, near_out, noises, w_scale, w_shift)
    far_row, near_row = swap(far_out, near_out, "sx")

    coded = (slots + CODE * here("sx")).transpose(2, 1, 0).reshape(OWN, degree)
    sides = pl.pallas_call(
        functools.partial(collect, degree),
        out_shape=like((2, SIDE, width), jnp.float32),
        in_specs=[vmem] * 2,
        out_specs=vmem,
        scratch_shapes=[pltpu.VMEM((2, PAD, LANES), jnp.float32)],
        compiler_params=limits(8),
        cost_estimate=cost(1 << 20, 1 << 25),
        name="collect",
    )(x, coded)

    wide = like((OWN, width), jnp.float32)
    halves = like((2 * EAST, width), jnp.float32)
    first, gains, links, four_links, own_sum = pl.pallas_call(
        functools.partial(begin, sizes),
        out_shape=(
            like((OWN, width)),
            like((2 * layers, width), jnp.float32),
            like((OWN, OUT)),
            like((4 * EAST, 2 * LANES)),
            wide,
        ),
        in_specs=[vmem] * 5,
        out_specs=(vmem,) * 5,
        scratch_shapes=[
            pltpu.VMEM((2,) + slots.shape, jnp.int32),
            pltpu.VMEM((8, 8, LANES), jnp.float32),
        ],
        compiler_params=limits(8),
        cost_estimate=cost(1 << 24, 1 << 24),
        name="begin",
    )(x, slots, noises, w_scale, w_shift)

    sent = pl.pallas_call(
        columns_out,
        out_shape=(like((SIDE, width)),) * 2,
        in_specs=[pl.BlockSpec(memory_space=pl.ANY)] * 2 + [vmem] * 3,
        out_specs=(vmem,) * 2,
        scratch_shapes=[pltpu.VMEM((2, SIDE, width), jnp.float32)],
        compiler_params=limits(8),
        cost_estimate=cost(1 << 20, 1 << 25),
        name="columns_out",
    )(w_out, gains, sides, far_row, near_row)
    far_column, near_column = swap(*sent, "sy")

    (
        end_sum, end_part, four_sum, two_part, two_x, mid, rim_rows, ring_rows, rim_x,
    ) = pl.pallas_call(
        functools.partial(prepare, sizes, degree),
        out_shape=(
            halves,
            halves,
            like((4 * EAST, width), jnp.float32),
            halves,
            halves,
            like((OWN, variables), jnp.float32),
            like((4 * NORTH, width)),
            like((2 * NORTH, ALL)),
            like((2 * NORTH, width), jnp.float32),
        ),
        in_specs=[vmem] * 11 + [pl.BlockSpec(memory_space=pl.ANY)],
        out_specs=(vmem,) * 9,
        scratch_shapes=[
            pltpu.VMEM((OWN + 2 * NORTH, width), jnp.bfloat16),
            pltpu.VMEM((OWN + 2 * NORTH, width), jnp.float32),
            pltpu.VMEM((ALL - OWN, width), jnp.bfloat16),
            pltpu.VMEM((OWN, width), jnp.float32),
        ],
        compiler_params=limits(16),
        cost_estimate=cost(1 << 24, 1 << 25),
        name="prepare",
    )(
        x, first, gains, links, own_sum, w_self, w_nbr, w_out, w_dec, far_row, near_row, sent[1]
    )

    busy = 2 * EAST + OUT - OWN
    preds, shares, _ = pl.pallas_call(
        functools.partial(advance, sizes, degree),
        out_shape=(like((OWN, variables)),) * 2 + (like(mid.shape, jnp.float32),),
        in_specs=[vmem] * 19,
        out_specs=(vmem,) * 3,
        input_output_aliases={8: 2},
        scratch_shapes=[
            pltpu.VMEM((ALL - OWN, width), jnp.bfloat16),
            pltpu.VMEM((2 * LANES, width), jnp.bfloat16),
            pltpu.VMEM((busy, width), jnp.bfloat16),
            pltpu.VMEM((busy, width), jnp.float32),
            pltpu.VMEM((OUT - OWN, ALL), jnp.bfloat16),
        ],
        compiler_params=limits(16),
        cost_estimate=cost(1 << 31, 1 << 23),
        name="advance",
    )(
        first, gains, four_links, end_sum, end_part, four_sum, two_part, two_x, mid,
        rim_rows, ring_rows, rim_x, sides, far_column, near_column, w_self, w_nbr, w_out, w_dec,
    )

    members = lax.axis_size("member")
    share = OWN // members
    mine = lax.all_to_all(shares.reshape(members, share, variables), "member", 0, 0)
    copies = pl.pallas_call(
        score_share,
        out_shape=like(mine.shape),
        in_specs=[vmem] * 2,
        out_specs=vmem,
        compiler_params=limits(8),
        name="score_share",
    )(mine, target.reshape(OWN, variables))
    scores = lax.all_to_all(copies, "member", 0, 0).astype(jnp.float32)
    return (preds.reshape(1, EAST, NORTH, variables), scores.reshape(target.shape))


def solution(mesh):
    placed = (
        P("member", "sx", "sy", None),
        P("member", None),
        P("sx", "sy", None),
        P("sx", "sy", None),
        P(),
        P(),
        P(),
        P(),
        P(),
        P(),
    )
    return jax.shard_map(
        local,
        mesh=mesh,
        in_specs=placed,
        out_specs=(P("member", "sx", "sy", None), P("sx", "sy", None)),
        check_vma=False,
    )
```
